256 devices in a mesh: prow: 8 (over y_hi, x), pcol: 32 (over z, y_lo, core).
Axes of the slice: x: 4, y: 4 (y_hi: 2, y_lo: 2; y = y_hi * 2 + y_lo), z: 8, core: 2. Of those that a mesh axis runs over, the one named last changes fastest.
Arguments:
- factor_panels: float32 [8, 4096, 512], P('prow', 'pcol'), may hold values from -0.046875 to 0.046875
- diag_inverse: float32 [8, 512, 512], P('prow'), as said below
- block_lists: int32 [8, 7], replicated, may hold values from 1 to 8, as said below
- parent: int32 [8], replicated, may hold values from 1 to 8, as said below
Outputs:
- inverse_blocks: float32 [8, 4096, 512], P('prow', 'pcol')
The draws below stay inside these ranges and needn't reach their ends.
Inputs may be any that keep to these rules, and one draw needn't show every extreme that they name: `block_lists`: row K lists in rising order the supernodes whose block rows are nonzero in factor column K, padded at the end with 8; every listed supernode is an ancestor of K, parent[K] is listed, and every other listed supernode is also listed for parent[K]; the last row is all padding. parent[K] > K; the last supernode is the root and has the value 8. `diag_inverse`: each block is symmetric.
All inputs are finite; a program needn't handle non-finite values.
Results may differ from the reference program's by a relative error of at most 0.0001.
Values sent between devices are 32-bit elements; how exact they have to be, the bound alone decides.
A program may use at most 64 MiB of HBM per device.

```python
import jax
import jax.numpy as jnp
from jax import lax

S = 512
NSUP = 8


def tree_tables(key):
    step_key, keep_key = jax.random.split(key)
    parent_step = jax.random.randint(step_key, (NSUP,), 1, 3)
    node_ids = jnp.arange(NSUP, dtype=jnp.int32)
    parent_ids = jnp.minimum(node_ids + parent_step, NSUP - 1)
    parent_ids = jnp.where(node_ids == NSUP - 1, NSUP, parent_ids).astype(jnp.int32)
    keep_bits = jax.random.randint(keep_key, (NSUP, NSUP), 0, 2)
    member = jnp.zeros((NSUP + 1, NSUP), jnp.int32)
    for target in range(NSUP - 2, -1, -1):
        parent_node = parent_ids[target]
        inherited = member[parent_node] * keep_bits[target]
        direct = (node_ids == parent_node).astype(jnp.int32)
        member = member.at[target].set(jnp.maximum(inherited, direct))
    scores = jnp.where(member[:NSUP] > 0, node_ids[None, :], NSUP + node_ids[None, :])
    ordered = jnp.sort(scores, axis=1)
    listed = jnp.where(ordered >= NSUP, NSUP, ordered)[:, :NSUP - 1]
    return (parent_ids, listed.astype(jnp.int32))


def draw_parent(key, part):
    parent_ids, listed = tree_tables(key)
    return parent_ids


def draw_block_lists(key, part):
    parent_ids, listed = tree_tables(key)
    return listed


def draw_diag_inverse(key, part):
    key = jax.random.fold_in(key, 7)
    scale_key, noise_key = jax.random.split(key)
    levels = jnp.exp(jax.random.uniform(scale_key, (NSUP, S), jnp.float32, jnp.log(0.5), jnp.log(2.0)))
    noise = jax.random.normal(noise_key, (NSUP, S, S), jnp.float32)
    symmetric = (noise + jnp.swapaxes(noise, 1, 2)) * (0.35 / jnp.sqrt(jnp.float32(S)))
    identity = jnp.eye(S, dtype=jnp.float32)
    return symmetric + identity[None, :, :] * levels[:, None, :]


def level_of(rng, extent, shards, least, largest):
    gain = 1.0
    for dim, blocks in shards:
        heights = jax.random.uniform(jax.random.fold_in(jax.random.fold_in(rng, 6), dim), (blocks,), jnp.float32, least / len(shards), largest / len(shards))
        gain = gain * jnp.repeat(jnp.exp(heights), extent[dim] // blocks).reshape((-1,) + (1,) * (len(extent) - 1 - dim))
    return gain


def normal_values(stream_key, shape, scale, limit, pieces=(), kind=jnp.bfloat16):
    result = scale * jax.random.normal(stream_key, shape, jnp.float32)
    if pieces:
        result = result * level_of(stream_key, shape, pieces, -0.22, 0.18)
    return jnp.clip(result, -limit, limit).astype(kind)


def setup_inputs(seed: int = 0) -> dict:
    splits = jax.random.split(jax.random.key(seed), 5)
    factor_panels = normal_values(splits[0], (NSUP, NSUP * S, S), (4 * S * NSUP) ** -0.5, 0.046875, ((0, 8), (1, 32)), jnp.float32)
    diag_inverse = draw_diag_inverse(jax.random.fold_in(splits[4], 71), 0)
    block_lists = draw_block_lists(jax.random.fold_in(splits[4], 71), 0)
    parent = draw_parent(jax.random.fold_in(splits[4], 71), 0)
    return dict(factor_panels=factor_panels, diag_inverse=diag_inverse, block_lists=block_lists, parent=parent)


def pattern_of(block_lists, parent, target):
    node_ids = jnp.arange(NSUP, dtype=jnp.int32)
    listed = jnp.any(block_lists[target][:, None] == node_ids[None, :], axis=0)
    return jnp.logical_or(listed, parent[target] == node_ids).astype(jnp.float32)


def reference(factor_panels, diag_inverse, block_lists, parent):
    factor_blocks = factor_panels.reshape(NSUP, NSUP, S, S)
    inverse = jnp.zeros((NSUP, NSUP, S, S), jnp.float32)
    for target in range(NSUP - 1, -1, -1):
        pattern_mask = pattern_of(block_lists, parent, target)
        panel = factor_blocks[:, target] * pattern_mask[:, None, None]
        product = jnp.einsum('jiab,jbk->iak', inverse, panel, precision=lax.Precision.HIGHEST)
        column_panel = -product * pattern_mask[:, None, None]
        diagonal = jnp.einsum('iba,ibk->ak', column_panel, panel, precision=lax.Precision.HIGHEST)
        inverse = inverse.at[target].set(column_panel)
        inverse = inverse.at[:, target].set(jnp.swapaxes(column_panel, 1, 2))
        inverse = inverse.at[target, target].set(diag_inverse[target] - diagonal)
    return inverse.reshape(NSUP, NSUP * S, S)
```

```python
import functools

import jax
import jax.numpy as jnp
from jax import lax
from jax.experimental import pallas as pl
from jax.experimental.pallas import tpu as pltpu
from jax.sharding import PartitionSpec as P

MESH = pl.DeviceIdType.MESH
NODES = 8
WIDTH = 512
SHARES = 4
ROWS = 128
CHUNKS = 2
PIECE = ROWS // CHUNKS


def pattern_weight(lists_ref, parent_ref, target, node):
    found = parent_ref[target] == node
    for i in range(NODES - 1):
        found = jnp.logical_or(found, lists_ref[target, i] == node)
    return jnp.where(found, 1.0, 0.0).astype(jnp.float32)


def split(value):
    high = value.astype(jnp.bfloat16)
    low = (value - high.astype(jnp.float32)).astype(jnp.bfloat16)
    return high, low


def product(left, high_ref, low_ref, transposed):
    high, low = split(left)
    dims = (((1,), (1 if transposed else 0,)), ((), ()))
    rows = left.shape[0]
    both = lax.dot_general(
        jnp.concatenate([high, low], 0), high_ref[...], dims, preferred_element_type=jnp.float32
    )
    cross = lax.dot_general(high, low_ref[...], dims, preferred_element_type=jnp.float32)
    return both[:rows] + both[rows:] + cross


def kernel(
    f_ref, d_ref, lists_ref, parent_ref, out_ref,
    raw, lhi, llo, dhi, dlo, mine, mrecv, zacc, psend, precv,
    z_send, z_recv, y_send, y_recv, c_send, c_recv, m_send, m_recv, p_send, p_recv,
):
    node = lax.axis_index("prow")
    col = lax.axis_index("pcol")
    plane = col // SHARES
    share = lax.rem(col, SHARES)
    y_low, core = share // 2, lax.rem(share, 2)
    y_share = (1 - y_low) * 2 + core

    def device(n, z, s):
        return (n, z * SHARES + s)

    barrier = pltpu.get_barrier_semaphore()
    for step in range(1, NODES):
        pl.semaphore_signal(
            barrier, device_id=device(lax.rem(node + step, NODES), plane, share), device_id_type=MESH
        )
        pl.semaphore_signal(
            barrier, device_id=device(node, lax.rem(plane + step, NODES), share), device_id_type=MESH
        )
    pl.semaphore_signal(barrier, device_id=device(node, plane, y_share), device_id_type=MESH)
    pl.semaphore_signal(
        barrier, device_id=device(node, plane, y_low * 2 + 1 - core), device_id_type=MESH
    )
    raw[plane, share] = f_ref[...] * pattern_weight(lists_ref, parent_ref, plane, node)
    high, low = split(d_ref[...])
    dhi[...] = high
    dlo[...] = low
    pl.semaphore_wait(barrier, 2 * (NODES - 1) + 2)

    def z_copy(k, target):
        return pltpu.make_async_remote_copy(
            src_ref=raw.at[k, share], dst_ref=raw.at[k, share],
            send_sem=z_send.at[target], recv_sem=z_recv.at[k],
            device_id=device(node, target, share), device_id_type=MESH,
        )

    def y_copy(k):
        return pltpu.make_async_remote_copy(
            src_ref=raw.at[k, share], dst_ref=raw.at[k, share],
            send_sem=y_send.at[k], recv_sem=y_recv.at[k],
            device_id=device(node, plane, y_share), device_id_type=MESH,
        )

    def c_copy(k, which):
        held = share if which == 0 else y_share
        return pltpu.make_async_remote_copy(
            src_ref=raw.at[k, held], dst_ref=raw.at[k, held],
            send_sem=c_send.at[k, which], recv_sem=c_recv.at[k, which],
            device_id=device(node, plane, y_low * 2 + 1 - core), device_id_type=MESH,
        )

    def m_copy(k, target, piece):
        return pltpu.make_async_remote_copy(
            src_ref=mine.at[piece], dst_ref=mrecv.at[k, piece],
            send_sem=m_send.at[target, piece], recv_sem=m_recv.at[k, piece],
            device_id=device(target, plane, share), device_id_type=MESH,
        )

    def p_copy(k, target, piece):
        return pltpu.make_async_remote_copy(
            src_ref=psend.at[target, piece], dst_ref=precv.at[k, piece],
            send_sem=p_send.at[target, piece], recv_sem=p_recv.at[k, piece],
            device_id=device(target, plane, share), device_id_type=MESH,
        )

    @pl.when(node > plane)
    def _():
        def body(target, carry):
            @pl.when(target != plane)
            def _():
                z_copy(plane, target).start()

            return carry

        lax.fori_loop(0, NODES, body, 0)

    def gather(k):
        @pl.when(k != plane)
        def _():
            z_copy(k, plane).wait_recv()

        y_copy(k).start()
        c_copy(k, 0).start()

    def relay(k):
        y_copy(k).wait_recv()
        c_copy(k, 1).start()

    def prepare(k):
        c_copy(k, 0).wait_recv()
        c_copy(k, 1).wait_recv()
        for i in range(SHARES):
            high, low = split(raw[k, i])
            lhi[k, i * ROWS : (i + 1) * ROWS] = high
            llo[k, i * ROWS : (i + 1) * ROWS] = low

    here = jnp.where(node == plane, 1.0, 0.0).astype(jnp.float32)
    for piece in range(CHUNKS):
        rows = lax.broadcasted_iota(jnp.int32, (PIECE, WIDTH), 0) + (share * ROWS + piece * PIECE)
        columns = lax.broadcasted_iota(jnp.int32, (PIECE, WIDTH), 1)
        unit = jnp.where(rows == columns, 1.0, 0.0).astype(jnp.float32)
        mrecv[plane, piece] = unit
        mine[piece] = unit * here

    @pl.when(node > 0)
    def _():
        gather(0)

    @pl.when(node > 1)
    def _():
        gather(1)

    @pl.when(node > 0)
    def _():
        relay(0)

    def forward_term(k, piece):
        @pl.when(k > plane)
        def _():
            m_copy(k, node, piece).wait_recv()

        mine[piece] = mine[piece] - product(mrecv[k, piece], lhi.at[k], llo.at[k], True)

    def forward(k, carry):
        @pl.when(k + 2 < node)
        def _():
            gather(k + 2)

        @pl.when(k + 1 < node)
        def _():
            relay(k + 1)

        prepare(k)

        @pl.when(jnp.logical_and(k >= plane, k < node - 1))
        def _():
            for piece in range(CHUNKS):
                forward_term(k, piece)

        return carry

    lax.fori_loop(0, node, forward, 0)

    @pl.when(node > plane)
    def _():
        for piece in range(CHUNKS):
            forward_term(node - 1, piece)

            def body(target, carry):
                m_copy(node, target, piece).start()
                return carry

            lax.fori_loop(node + 1, NODES, body, 0)

    for piece in range(CHUNKS):
        zacc[piece] = product(mine[piece], dhi, dlo, False)

    def collect(k, piece):
        p_copy(k, node, piece).wait_recv()
        zacc[piece] = zacc[piece] - precv[k, piece]

    def spread(target, piece):
        psend[target, piece] = product(zacc[piece], lhi.at[target], llo.at[target], False)
        p_copy(node, target, piece).start()

    def backward(i, carry):
        for piece in range(CHUNKS):
            collect(NODES - 1 - i, piece)
        return carry

    lax.fori_loop(0, NODES - 2 - node, backward, 0)

    for piece in range(CHUNKS):
        @pl.when(node < NODES - 1)
        def _():
            collect(node + 1, piece)

        @pl.when(node > 0)
        def _():
            spread(node - 1, piece)

    def remaining(i, carry):
        for piece in range(CHUNKS):
            spread(node - 2 - i, piece)
        return carry

    lax.fori_loop(0, node - 1, remaining, 0)

    low_node, high_node = jnp.minimum(node, plane), jnp.maximum(node, plane)
    weight = pattern_weight(lists_ref, parent_ref, low_node, high_node)
    weight = jnp.where(node == plane, 1.0, weight)
    for piece in range(CHUNKS):
        out_ref[piece * PIECE : (piece + 1) * PIECE] = zacc[piece] * weight

    def drain_row(k, carry):
        y_copy(k).wait_send()
        c_copy(k, 0).wait_send()
        c_copy(k, 1).wait_send()
        for piece in range(CHUNKS):
            p_copy(node, k, piece).wait_send()
        return carry

    lax.fori_loop(0, node, drain_row, 0)

    @pl.when(node > plane)
    def _():
        def drain_z(target, carry):
            @pl.when(target != plane)
            def _():
                z_copy(plane, target).wait_send()

            return carry

        lax.fori_loop(0, NODES, drain_z, 0)

        def drain_m(target, carry):
            for piece in range(CHUNKS):
                m_copy(node, target, piece).wait_send()
            return carry

        lax.fori_loop(node + 1, NODES, drain_m, 0)


def shards(factor_panels, diag_inverse, block_lists, parent):
    f32, bf16 = jnp.float32, jnp.bfloat16
    dma = pltpu.SemaphoreType.DMA
    vmem = pl.BlockSpec(memory_space=pltpu.VMEM)
    smem = pl.BlockSpec(memory_space=pltpu.SMEM)
    inverse = pl.pallas_call(
        kernel,
        out_shape=jax.ShapeDtypeStruct((ROWS, WIDTH), f32),
        in_specs=[vmem, vmem, smem, smem],
        out_specs=vmem,
        scratch_shapes=[
            pltpu.VMEM((NODES, SHARES, ROWS, WIDTH), f32),
            pltpu.VMEM((NODES, WIDTH, WIDTH), bf16),
            pltpu.VMEM((NODES, WIDTH, WIDTH), bf16),
            pltpu.VMEM((WIDTH, WIDTH), bf16),
            pltpu.VMEM((WIDTH, WIDTH), bf16),
            pltpu.VMEM((CHUNKS, PIECE, WIDTH), f32),
            pltpu.VMEM((NODES, CHUNKS, PIECE, WIDTH), f32),
            pltpu.VMEM((CHUNKS, PIECE, WIDTH), f32),
            pltpu.VMEM((NODES, CHUNKS, PIECE, WIDTH), f32),
            pltpu.VMEM((NODES, CHUNKS, PIECE, WIDTH), f32),
            dma((NODES,)), dma((NODES,)), dma((NODES,)), dma((NODES,)),
            dma((NODES, 2)), dma((NODES, 2)),
            dma((NODES, CHUNKS)), dma((NODES, CHUNKS)), dma((NODES, CHUNKS)), dma((NODES, CHUNKS)),
        ],
        compiler_params=pltpu.CompilerParams(
            collective_id=0, has_side_effects=True, vmem_limit_bytes=48 * 2**20
        ),
        name="selected_inverse",
    )(factor_panels[0], diag_inverse[0], block_lists, parent)
    return inverse[None]


def solution(mesh):
    placed = (P("prow", "pcol", None), P("prow", None, None), P(), P())
    return jax.shard_map(
        shards, mesh=mesh, in_specs=placed, out_specs=P("prow", "pcol", None), check_vma=False
    )
```

```python
import jax
import jax.numpy as jnp
from jax import lax
from jax.experimental import pallas as pl
from jax.experimental.pallas import tpu as pltpu
from jax.sharding import PartitionSpec as P

MESH = pl.DeviceIdType.MESH
NODES = 8
WIDTH = 512
SHARES = 4
ROWS = 128
HALF = ROWS // 2
SUBS = 2
PIECE = HALF // SUBS
AHEAD, BEHIND = 4, 3


def pattern_weight(lists_ref, parent_ref, target, node):
    found = parent_ref[target] == node
    for i in range(NODES - 1):
        found = jnp.logical_or(found, lists_ref[target, i] == node)
    return jnp.where(found, 1.0, 0.0).astype(jnp.float32)


def split(value):
    high = value.astype(jnp.bfloat16)
    low = (value - high.astype(jnp.float32)).astype(jnp.bfloat16)
    return high, low


def product(left, high_ref, low_ref, transposed):
    high, low = split(left)
    dims = (((1,), (1 if transposed else 0,)), ((), ()))
    rows = left.shape[0]
    both = lax.dot_general(
        jnp.concatenate([high, low], 0), high_ref[...], dims, preferred_element_type=jnp.float32
    )
    cross = lax.dot_general(high, low_ref[...], dims, preferred_element_type=jnp.float32)
    return both[:rows] + both[rows:] + cross


def kernel(
    f_hbm, d_hbm, lists_hbm, parent_hbm, out_ref,
    f_ref, d_ref, lists_ref, parent_ref,
    raw, lhi, llo, dhi, dlo, mine, mrecv, zacc, psend, precv, xrecv, across, trecv,
    in_sem, z_send, z_recv, y_send, y_recv, c_send, c_recv,
    m_send, m_recv, p_send, p_recv, x_send, x_recv, a_send, a_recv, t_send, t_recv,
):
    node = lax.axis_index("prow")
    col = lax.axis_index("pcol")
    plane = col // SHARES
    share = lax.rem(col, SHARES)
    y_low, core = share // 2, lax.rem(share, 2)
    y_share = (1 - y_low) * 2 + core
    c_share = y_low * 2 + 1 - core
    upper = plane // (NODES // 2)
    mirror = NODES - 1 - plane
    blocks = (jnp.minimum(plane, mirror), jnp.maximum(plane, mirror))

    def device(n, z, s):
        return (n, z * SHARES + s)

    barrier = pltpu.get_barrier_semaphore()

    def greet(target):
        pl.semaphore_signal(barrier, device_id=target, device_id_type=MESH)

    for step in range(1, NODES):
        greet(device(lax.rem(node + step, NODES), plane, share))
    greet(device(node, lax.rem(plane + 1, NODES), share))
    greet(device(node, lax.rem(plane + NODES - 1, NODES), share))
    greet(device(node, mirror, share))
    greet(device(node, plane, y_share))
    greet(device(node, plane, c_share))

    @pl.when(node < plane)
    def _():
        for s in range(SHARES):
            greet(device(plane, plane, s))

    @pl.when(node == plane)
    def _():
        for step in range(1, NODES):
            greet(device(node, lax.rem(plane + step, NODES), share))


    loads = [
        pltpu.make_async_copy(src, dst, in_sem.at[i])
        for i, (src, dst) in enumerate(
            [(lists_hbm, lists_ref), (parent_hbm, parent_ref), (f_hbm, f_ref), (d_hbm, d_ref)]
        )
    ]
    for load in loads:
        load.start()
    for load in loads[:3]:
        load.wait()
    raw[plane, share] = f_ref[...] * pattern_weight(lists_ref, parent_ref, plane, node)
    for h in range(2):
        first = share * ROWS + upper * HALF
        rows = lax.broadcasted_iota(jnp.int32, (HALF, WIDTH), 0) + first
        columns = lax.broadcasted_iota(jnp.int32, (HALF, WIDTH), 1)
        unit = jnp.where(rows == columns, 1.0, 0.0).astype(jnp.float32)
        here = jnp.where(node == blocks[h], 1.0, 0.0).astype(jnp.float32)
        mrecv[blocks[h], h] = unit
        mine[h] = unit * here
    loads[3].wait()
    high, low = split(d_ref[...])
    dhi[...] = high
    dlo[...] = low
    greeted = NODES - 1 + 5 + jnp.where(node == plane, SHARES * node, 1)
    pl.semaphore_wait(barrier, greeted)

    def remote(src, dst, send, recv, target):
        return pltpu.make_async_remote_copy(
            src_ref=src, dst_ref=dst, send_sem=send, recv_sem=recv,
            device_id=target, device_id_type=MESH,
        )

    def z_copy(k, sub, way):
        step = 1 if way == 0 else NODES - 1
        here = raw.at[k, share, pl.ds(sub * HALF, HALF)]
        target = device(node, lax.rem(plane + step, NODES), share)
        return remote(here, here, z_send.at[k, sub, way], z_recv.at[k, sub], target)

    def y_copy(k, sub):
        here = raw.at[k, share, pl.ds(sub * HALF, HALF)]
        target = device(node, plane, y_share)
        return remote(here, here, y_send.at[k, sub], y_recv.at[k, sub], target)

    def c_copy(k, sub, which):
        here = raw.at[k, share if which == 0 else y_share, pl.ds(sub * HALF, HALF)]
        target = device(node, plane, c_share)
        return remote(here, here, c_send.at[k, sub, which], c_recv.at[k, sub, which], target)

    def part(ref, index, h, sub):
        if sub is None:
            return ref.at[index, h] if index is not None else ref.at[h]
        rows = pl.ds(sub * PIECE, PIECE)
        return ref.at[index, h, rows] if index is not None else ref.at[h, rows]

    def m_copy(k, target, h, sub):
        i = sub or 0
        return remote(
            part(mine, None, h, sub), part(mrecv, k, h, sub),
            m_send.at[target, h, i], m_recv.at[k, h, i], device(target, plane, share),
        )

    def p_copy(k, target, h, sub):
        i = sub or 0
        return remote(
            part(psend, target, h, sub), part(precv, k, h, sub),
            p_send.at[target, h, i], p_recv.at[k, h, i], device(target, plane, share),
        )

    def passes(k, way, distance):
        if distance > (BEHIND if way else AHEAD):
            return False
        if way == 0:
            return jnp.logical_and(k < node, k >= 2)
        return jnp.logical_and(k < node, jnp.logical_or(k >= 1, distance <= 1))

    def ring(distance):
        ways = [0, 1] if distance else [0]
        return [(way, lax.rem(plane + (distance if way else NODES - distance), NODES)) for way in ways]

    def each(distance, action):
        for way, k in ring(distance):
            if distance == 0 or passes(k, way, distance) is not False:
                @pl.when(jnp.logical_and(k < node, k >= blocks[0]))
                def _():
                    for sub in range(SUBS):
                        action(k, sub)

    def sends(distance, sub, action):
        for way, k in ring(distance):
            for onward in ([0, 1] if distance == 0 else [way]):
                further = passes(k, onward, distance + 1)
                if further is not False:
                    @pl.when(further)
                    def _():
                        action(k, sub, onward)

    def land(distance):
        for sub in range(SUBS):
            for way, k in ring(distance):
                arrives = passes(k, way, distance) if distance else False
                if arrives is not False:
                    @pl.when(arrives)
                    def _():
                        z_copy(k, sub, way).wait_recv()

            sends(distance, sub, lambda k, i, way: z_copy(k, i, way).start())
            for way, k in ring(distance):
                if distance == 0 or passes(k, way, distance) is not False:
                    @pl.when(jnp.logical_and(k < node, k >= blocks[0]))
                    def _():
                        y_copy(k, sub).start()
                        c_copy(k, sub, 0).start()

    def relay(k, sub):
        y_copy(k, sub).wait_recv()
        c_copy(k, sub, 1).start()

    def prepare(k, sub):
        c_copy(k, sub, 0).wait_recv()
        c_copy(k, sub, 1).wait_recv()
        for i in range(SHARES):
            high, low = split(raw[k, i, sub * HALF : (sub + 1) * HALF])
            rows = slice(i * ROWS + sub * HALF, i * ROWS + (sub + 1) * HALF)
            lhi[k, rows] = high
            llo[k, rows] = low

    for step in range(AHEAD + 3):
        if step <= AHEAD:
            land(step)
        if 1 <= step <= AHEAD + 1:
            each(step - 1, relay)
        if 2 <= step:
            each(step - 2, prepare)

    def forward(k, carry):
        for h in range(2):
            @pl.when(k >= blocks[h])
            def _():
                @pl.when(k > blocks[h])
                def _():
                    m_copy(k, node, h, None).wait_recv()

                mine[h] = mine[h] - product(mrecv[k, h], lhi.at[k], llo.at[k], True)

        return carry

    lax.fori_loop(0, node - 1, forward, 0)

    for h in range(2):
        @pl.when(node > blocks[h])
        def _():
            last = node - 1
            for sub in range(SUBS):
                @pl.when(last > blocks[h])
                def _():
                    m_copy(last, node, h, sub).wait_recv()

                rows = slice(sub * PIECE, (sub + 1) * PIECE)
                mine[h, rows] = mine[h, rows] - product(
                    mrecv[last, h, rows], lhi.at[last], llo.at[last], True
                )

                @pl.when(node < NODES - 1)
                def _():
                    m_copy(node, node + 1, h, sub).start()

            def body(target, carry):
                m_copy(node, target, h, None).start()
                return carry

            lax.fori_loop(node + 2, NODES, body, 0)

    for h in range(2):
        zacc[h] = product(mine[h], dhi, dlo, False)

    def collect(k, h, sub):
        p_copy(k, node, h, sub).wait_recv()
        rows = slice(0, HALF) if sub is None else slice(sub * PIECE, (sub + 1) * PIECE)
        zacc[h, rows] = zacc[h, rows] - precv[k, h, rows]

    def spread(to, h, sub):
        rows = slice(0, HALF) if sub is None else slice(sub * PIECE, (sub + 1) * PIECE)
        psend[to, h, rows] = product(zacc[h, rows], lhi.at[to], llo.at[to], False)
        p_copy(node, to, h, sub).start()

    for h in (1, 0):
        @pl.when(node >= blocks[h])
        def _():
            def backward(i, carry):
                collect(NODES - 1 - i, h, None)
                return carry

            lax.fori_loop(0, NODES - 2 - node, backward, 0)
            for sub in range(SUBS):
                @pl.when(node < NODES - 1)
                def _():
                    collect(node + 1, h, sub)

                @pl.when(node > blocks[h])
                def _():
                    spread(node - 1, h, sub)

    for h in (0, 1):
        def remaining(i, carry):
            spread(node - 2 - i, h, None)
            return carry

        lax.fori_loop(0, node - 1 - blocks[h], remaining, 0)

    for h in range(2):
        weight = pattern_weight(lists_ref, parent_ref, blocks[h], node)
        zacc[h] = zacc[h] * jnp.where(node == blocks[h], 1.0, weight)

    kept, sent = upper, 1 - upper

    def x_copy():
        target = device(node, mirror, share)
        return remote(zacc.at[sent], xrecv, x_send, x_recv, target)

    def a_copy(h):
        target = device(node, node, share)
        return remote(zacc.at[h], across.at[blocks[h], upper], a_send.at[h], a_recv.at[blocks[h], upper], target)

    def t_copy(k, half, s):
        columns = pl.ds(s * ROWS, ROWS)
        return remote(
            across.at[k, half, slice(None), columns], trecv.at[share, half],
            t_send.at[k, half, s], t_recv.at[share, half], device(k, plane, s),
        )

    def arrival(s, half):
        tile = trecv.at[s, half]
        return remote(tile, tile, t_send.at[0, 0, 0], t_recv.at[s, half], device(plane, plane, s))

    @pl.when(node >= mirror)
    def _():
        x_copy().start()

    for h in range(2):
        @pl.when(jnp.logical_and(node > blocks[h], node != plane))
        def _():
            a_copy(h).start()

        @pl.when(jnp.logical_and(node > blocks[h], node == plane))
        def _():
            across[blocks[h], upper] = zacc[h]

    @pl.when(node >= plane)
    def _():
        out_ref[pl.ds(upper * HALF, HALF)] = zacc[kept]
        x_copy().wait_recv()
        out_ref[pl.ds((1 - upper) * HALF, HALF)] = xrecv[...]

    @pl.when(node == plane)
    def _():
        def deal(i, carry):
            k = node - 1 - i
            for half in range(2):
                source = jnp.minimum(k, NODES - 1 - k) if half == 0 else jnp.maximum(k, NODES - 1 - k)

                @pl.when(source != plane)
                def _():
                    into = across.at[k, half]
                    remote(into, into, a_send.at[0], a_recv.at[k, half], device(node, source, share)).wait_recv()

                for s in range(SHARES):
                    t_copy(k, half, s).start()
            return carry

        lax.fori_loop(0, node, deal, 0)

    @pl.when(node < plane)
    def _():
        for s in range(SHARES):
            for half in range(2):
                arrival(s, half).wait_recv()
        for s in range(SHARES):
            tiles = jnp.concatenate([trecv[s, 0], trecv[s, 1]], 0)
            out_ref[:, s * ROWS : (s + 1) * ROWS] = tiles.T

    @pl.when(node >= mirror)
    def _():
        x_copy().wait_send()

    @pl.when(node == plane)
    def _():
        def drain_t(k, carry):
            for half in range(2):
                for s in range(SHARES):
                    t_copy(k, half, s).wait_send()
            return carry

        lax.fori_loop(0, node, drain_t, 0)

    for distance in range(AHEAD + 1):
        def drained(k, sub):
            y_copy(k, sub).wait_send()
            c_copy(k, sub, 0).wait_send()
            c_copy(k, sub, 1).wait_send()

        each(distance, drained)
        for sub in range(SUBS):
            sends(distance, sub, lambda k, i, way: z_copy(k, i, way).wait_send())

    for h in range(2):
        @pl.when(node > blocks[h])
        def _():
            @pl.when(node != plane)
            def _():
                a_copy(h).wait_send()

            for sub in range(SUBS):
                p_copy(node, node - 1, h, sub).wait_send()

                @pl.when(node < NODES - 1)
                def _():
                    m_copy(node, node + 1, h, sub).wait_send()

        def drain_m(target, carry):
            m_copy(node, target, h, None).wait_send()
            return carry

        def drain_p(target, carry):
            p_copy(node, target, h, None).wait_send()
            return carry

        lax.fori_loop(node + 2, jnp.where(node > blocks[h], NODES, 0), drain_m, 0)
        lax.fori_loop(blocks[h], node - 1, drain_p, 0)


def shards(factor_panels, diag_inverse, block_lists, parent):
    f32, bf16, i32 = jnp.float32, jnp.bfloat16, jnp.int32
    dma = pltpu.SemaphoreType.DMA
    anywhere = pl.BlockSpec(memory_space=pl.ANY)
    messages = pltpu.VMEM((NODES, 2, HALF, WIDTH), f32)
    pair = pltpu.VMEM((2, HALF, WIDTH), f32)
    half = pltpu.VMEM((HALF, WIDTH), f32)
    row = pltpu.VMEM((NODES, WIDTH, WIDTH), bf16)
    block = pltpu.VMEM((WIDTH, WIDTH), bf16)
    flags = dma((NODES, 2, 2))
    inverse = pl.pallas_call(
        kernel,
        out_shape=jax.ShapeDtypeStruct((ROWS, WIDTH), f32),
        in_specs=[anywhere] * 4,
        out_specs=pl.BlockSpec(memory_space=pltpu.VMEM),
        scratch_shapes=[
            pltpu.VMEM((ROWS, WIDTH), f32), pltpu.VMEM((WIDTH, WIDTH), f32),
            pltpu.SMEM((NODES, NODES - 1), i32), pltpu.SMEM((NODES,), i32),
            pltpu.VMEM((NODES, SHARES, ROWS, WIDTH), f32),
            row, row, block, block, pair, messages, pair, messages, messages, half,
            messages, pltpu.VMEM((SHARES, 2, HALF, ROWS), f32),
            dma((4,)), flags, dma((NODES, SUBS)), dma((NODES, SUBS)), dma((NODES, SUBS)),
            flags, flags,
            flags, flags, flags, flags, dma(()), dma(()), dma((2,)), dma((NODES, 2)),
            dma((NODES, 2, SHARES)), dma((SHARES, 2)),
        ],
        compiler_params=pltpu.CompilerParams(
            collective_id=0, has_side_effects=True, vmem_limit_bytes=60 * 2**20
        ),
        name="selected_inverse",
    )(factor_panels[0], diag_inverse[0], block_lists, parent)
    return inverse[None]


def solution(mesh):
    placed = (P("prow", "pcol", None), P("prow", None, None), P(), P())
    return jax.shard_map(
        shards, mesh=mesh, in_specs=placed, out_specs=P("prow", "pcol", None), check_vma=False
    )
```

```python
import jax
import jax.numpy as jnp
from jax import lax
from jax.experimental import pallas as pl
from jax.experimental.pallas import tpu as pltpu
from jax.sharding import PartitionSpec as P

MESH = pl.DeviceIdType.MESH
NODES = 8
WIDTH = 512
SHARES = 4
ROWS = 128
HALF = ROWS // 2
SUBS = 2
PIECE = HALF // SUBS
DIRECT = 3
AHEAD, BEHIND = 4, 3
KEPT = 5
RELAY, PREPARE = 3, 4


def pattern_weight(lists_ref, parent_ref, target, node):
    found = parent_ref[target] == node
    for i in range(NODES - 1):
        found = jnp.logical_or(found, lists_ref[target, i] == node)
    return jnp.where(found, 1.0, 0.0).astype(jnp.float32)


def split(value):
    high = value.astype(jnp.bfloat16)
    low = (value - high.astype(jnp.float32)).astype(jnp.bfloat16)
    return high, low


def product(left, high_ref, low_ref, transposed):
    high, low = split(left)
    dims = (((1,), (1 if transposed else 0,)), ((), ()))
    rows = left.shape[0]
    both = lax.dot_general(
        jnp.concatenate([high, low], 0), high_ref[...], dims, preferred_element_type=jnp.float32
    )
    cross = lax.dot_general(high, low_ref[...], dims, preferred_element_type=jnp.float32)
    return both[:rows] + both[rows:] + cross


def kernel(
    f_hbm, d_hbm, lists_hbm, parent_hbm, out_ref,
    f_ref, d_ref, lists_ref, parent_ref,
    raw, lhi, llo, dhi, dlo, mine, mrecv, zacc, psend, precv, xrecv, across, trecv,
    scaled, part_sum, part_recv, solved,
    in_sem, z_send, z_recv, y_send, y_recv, c_send, c_recv,
    h_send, h_recv, s_send, s_recv, v_send, v_recv,
    m_send, m_recv, p_send, p_recv, x_send, x_recv, a_send, a_recv, t_send, t_recv,
):
    node = lax.axis_index("prow")
    col = lax.axis_index("pcol")
    plane = col // SHARES
    share = lax.rem(col, SHARES)
    y_low, core = share // 2, lax.rem(share, 2)
    y_share = (1 - y_low) * 2 + core
    c_share = y_low * 2 + 1 - core
    upper = plane // (NODES // 2)
    mirror = NODES - 1 - plane
    blocks = (jnp.minimum(plane, mirror), jnp.maximum(plane, mirror))
    first = jnp.maximum(node - KEPT, 0)
    friend = NODES - 1 - node
    helped = NODES - 1 - KEPT - node

    def device(n, z, s):
        return (n, z * SHARES + s)

    barrier = pltpu.get_barrier_semaphore()

    def greet(target):
        pl.semaphore_signal(barrier, device_id=target, device_id_type=MESH)

    for step in range(1, NODES):
        greet(device(lax.rem(node + step, NODES), plane, share))
    greet(device(node, lax.rem(plane + 1, NODES), share))
    greet(device(node, lax.rem(plane + NODES - 1, NODES), share))
    greet(device(node, mirror, share))
    greet(device(node, plane, y_share))
    greet(device(node, plane, c_share))

    @pl.when(node < plane)
    def _():
        @pl.when(plane > DIRECT)
        def _():
            for s in range(SHARES):
                greet(device(plane, plane, s))

        @pl.when(plane <= DIRECT)
        def _():
            for s in range(SHARES):
                greet(device(plane, node, s))
                greet(device(plane, NODES - 1 - node, s))

    @pl.when(jnp.logical_and(node == plane, node > DIRECT))
    def _():
        for step in range(1, NODES):
            greet(device(node, lax.rem(plane + step, NODES), share))


    loads = [
        pltpu.make_async_copy(src, dst, in_sem.at[i])
        for i, (src, dst) in enumerate(
            [(lists_hbm, lists_ref), (parent_hbm, parent_ref), (f_hbm, f_ref), (d_hbm, d_ref)]
        )
    ]
    for load in loads:
        load.start()
    for load in loads[:3]:
        load.wait()

    @pl.when(plane < node)
    def _():
        raw[plane, share] = f_ref[...] * pattern_weight(lists_ref, parent_ref, plane, node)

    for h in range(2):
        offset = share * ROWS + upper * HALF
        rows = lax.broadcasted_iota(jnp.int32, (HALF, WIDTH), 0) + offset
        columns = lax.broadcasted_iota(jnp.int32, (HALF, WIDTH), 1)
        unit = jnp.where(rows == columns, 1.0, 0.0).astype(jnp.float32)
        here = jnp.where(node == blocks[h], 1.0, 0.0).astype(jnp.float32)
        mrecv[blocks[h], h] = unit
        mine[h] = unit * here
    weights = []
    for h in range(2):
        weight = pattern_weight(lists_ref, parent_ref, blocks[h], node)
        weights.append(jnp.where(node == blocks[h], 1.0, weight))
    loads[3].wait()
    high, low = split(d_ref[...])
    dhi[...] = high
    dlo[...] = low
    relayed = jnp.where(node == plane, SHARES * node, 1)
    direct = SHARES * sum(jnp.where(node > blocks[h], 1, 0) for h in range(2))
    greeted = NODES - 1 + 5 + jnp.where(node > DIRECT, relayed, direct)
    pl.semaphore_wait(barrier, greeted)

    def remote(src, dst, send, recv, target):
        return pltpu.make_async_remote_copy(
            src_ref=src, dst_ref=dst, send_sem=send, recv_sem=recv,
            device_id=target, device_id_type=MESH,
        )

    def z_copy(k, sub, way):
        step = 1 if way == 0 else NODES - 1
        here = raw.at[k, share, pl.ds(sub * HALF, HALF)]
        target = device(node, lax.rem(plane + step, NODES), share)
        return remote(here, here, z_send.at[k, sub, way], z_recv.at[k, sub], target)

    def y_copy(k, sub):
        here = raw.at[k, share, pl.ds(sub * HALF, HALF)]
        target = device(node, plane, y_share)
        return remote(here, here, y_send.at[k, sub], y_recv.at[k, sub], target)

    def c_copy(k, sub, which):
        here = raw.at[k, share if which == 0 else y_share, pl.ds(sub * HALF, HALF)]
        target = device(node, plane, c_share)
        return remote(here, here, c_send.at[k, sub, which], c_recv.at[k, sub, which], target)

    def part(ref, index, h, sub):
        if sub is None:
            return ref.at[index, h] if index is not None else ref.at[h]
        rows = pl.ds(sub * PIECE, PIECE)
        return ref.at[index, h, rows] if index is not None else ref.at[h, rows]

    def m_copy(k, target, h, sub):
        i = sub or 0
        return remote(
            part(mine, None, h, sub), part(mrecv, k, h, sub),
            m_send.at[target, h, i], m_recv.at[k, h, i], device(target, plane, share),
        )

    def p_copy(k, target, h, sub):
        i = sub or 0
        return remote(
            part(psend, target, h, sub), part(precv, k, h, sub),
            p_send.at[target, h, i], p_recv.at[k, h, i], device(target, plane, share),
        )

    def member(k, kind):
        return k < helped if kind else jnp.logical_and(k >= first, k < node)

    def used(k, kind):
        return jnp.logical_and(member(k, kind), k >= blocks[0])

    def passes(k, way, distance, kind):
        if distance > (BEHIND if way else AHEAD):
            return False
        if way == 0:
            return jnp.logical_and(member(k, kind), k >= 2)
        return jnp.logical_and(member(k, kind), jnp.logical_or(k >= 1, distance <= 1))

    def ring(distance):
        ways = [0, 1] if distance else [0]
        return [(way, lax.rem(plane + (distance if way else NODES - distance), NODES)) for way in ways]

    def each(distance, kind, action):
        for way, k in ring(distance):
            if distance == 0 or passes(k, way, distance, kind) is not False:
                @pl.when(used(k, kind))
                def _():
                    for sub in range(SUBS):
                        action(k, k + KEPT * kind, sub)

    def sends(distance, sub, kind, action):
        for way, k in ring(distance):
            for onward in ([0, 1] if distance == 0 else [way]):
                further = passes(k, onward, distance + 1, kind)
                if further is not False:
                    @pl.when(further)
                    def _():
                        action(k, k + KEPT * kind, sub, onward)

    def land(distance, kind):
        for sub in range(SUBS):
            for way, k in ring(distance):
                arrives = passes(k, way, distance, kind) if distance else False
                if arrives is not False:
                    @pl.when(arrives)
                    def _():
                        z_copy(k + KEPT * kind, sub, way).wait_recv()

            sends(distance, sub, kind, lambda k, slot, i, way: z_copy(slot, i, way).start())
            for way, k in ring(distance):
                if distance == 0 or passes(k, way, distance, kind) is not False:
                    @pl.when(used(k, kind))
                    def _():
                        y_copy(k + KEPT * kind, sub).start()
                        c_copy(k + KEPT * kind, sub, 0).start()

    def relay(distance, kind):
        def action(k, slot, sub):
            y_copy(slot, sub).wait_recv()
            c_copy(slot, sub, 1).start()

        each(distance, kind, action)

    def prepare(k, slot, sub):
        c_copy(slot, sub, 0).wait_recv()
        c_copy(slot, sub, 1).wait_recv()
        for i in range(SHARES):
            high, low = split(raw[slot, i, sub * HALF : (sub + 1) * HALF])
            rows = slice(i * ROWS + sub * HALF, i * ROWS + (sub + 1) * HALF)
            lhi[slot, rows] = high
            llo[slot, rows] = low

    def gather(kind):
        for step in range(AHEAD + 1 + PREPARE):
            if step <= AHEAD:
                land(step, kind)
            if 0 <= step - RELAY <= AHEAD:
                relay(step - RELAY, kind)
            if 0 <= step - PREPARE <= AHEAD:
                each(step - PREPARE, kind, prepare)

    def hand_over():
        target = device(friend, plane, share)
        return remote(raw.at[plane, share], raw.at[plane + KEPT, share], h_send, h_recv, target)

    @pl.when(plane < first)
    def _():
        hand_over().start()

    gather(0)

    def forward(k, carry):
        for h in range(2):
            @pl.when(k >= blocks[h])
            def _():
                @pl.when(k > blocks[h])
                def _():
                    m_copy(k, node, h, None).wait_recv()

                mine[h] = mine[h] - product(mrecv[k, h], lhi.at[k], llo.at[k], True)

        return carry

    lax.fori_loop(first, node - 1, forward, 0)

    def s_copy():
        return remote(part_sum, part_recv, s_send, s_recv, device(friend, plane, share))

    @pl.when(blocks[0] < first)
    def _():
        s_copy().wait_recv()
        mine[0] = mine[0] - part_recv[...]

    for h in range(2):
        @pl.when(node > blocks[h])
        def _():
            last = node - 1
            for sub in range(SUBS):
                @pl.when(last > blocks[h])
                def _():
                    m_copy(last, node, h, sub).wait_recv()

                rows = slice(sub * PIECE, (sub + 1) * PIECE)
                mine[h, rows] = mine[h, rows] - product(
                    mrecv[last, h, rows], lhi.at[last], llo.at[last], True
                )

                @pl.when(node < NODES - 1)
                def _():
                    m_copy(node, node + 1, h, sub).start()

            def body(target, carry):
                m_copy(node, target, h, None).start()
                return carry

            lax.fori_loop(node + 2, jnp.minimum(node + KEPT + 1, NODES), body, 0)

    @pl.when(jnp.logical_and(node > blocks[0], jnp.logical_and(node >= 1, node <= NODES - 2 - KEPT)))
    def _():
        m_copy(node, 0, 0, None).start()
        mrecv[node, 0] = mine[0]

    @pl.when(plane < helped)
    def _():
        remote(raw.at[0, 0], raw.at[0, 0], h_send, h_recv, device(friend, plane, share)).wait_recv()

    gather(1)

    @pl.when(blocks[0] < helped)
    def _():
        part_sum[...] = jnp.zeros_like(part_sum)

        def term(k, carry):
            @pl.when(jnp.logical_and(k > blocks[0], k != node))
            def _():
                m_copy(k, node, 0, None).wait_recv()

            part_sum[...] += product(mrecv[k, 0], lhi.at[k + KEPT], llo.at[k + KEPT], True)
            return carry

        lax.fori_loop(blocks[0], helped, term, 0)
        s_copy().start()

    for h in range(2):
        zacc[h] = product(mine[h], dhi, dlo, False)

    def v_copy():
        return remote(zacc.at[0], solved, v_send, v_recv, device(friend, plane, share))

    def early_copy(to):
        return remote(
            psend.at[to + KEPT, 0], precv.at[friend, 0],
            p_send.at[to + KEPT, 0, 0], p_recv.at[friend, 0, 0], device(to, plane, share),
        )

    @pl.when(blocks[0] < helped)
    def _():
        v_copy().wait_recv()

        def early(to, carry):
            psend[to + KEPT, 0] = product(solved[...], lhi.at[to + KEPT], llo.at[to + KEPT], False)

            @pl.when(to != node)
            def _():
                early_copy(to).start()

            @pl.when(to == node)
            def _():
                precv[friend, 0] = psend[to + KEPT, 0]

            return carry

        lax.fori_loop(blocks[0], helped, early, 0)

    def collect(k, h, sub):
        if h == 0 and sub is None:
            @pl.when(jnp.logical_not(jnp.logical_and(k == friend, node < helped)))
            def _():
                p_copy(k, node, h, sub).wait_recv()
        else:
            p_copy(k, node, h, sub).wait_recv()
        rows = slice(0, HALF) if sub is None else slice(sub * PIECE, (sub + 1) * PIECE)
        zacc[h, rows] = zacc[h, rows] - precv[k, h, rows]

    def spread(to, h, sub):
        rows = slice(0, HALF) if sub is None else slice(sub * PIECE, (sub + 1) * PIECE)
        psend[to, h, rows] = product(zacc[h, rows], lhi.at[to], llo.at[to], False)
        p_copy(node, to, h, sub).start()

    for h in (1, 0):
        @pl.when(node >= blocks[h])
        def _():
            def backward(i, carry):
                collect(NODES - 1 - i, h, None)
                return carry

            lax.fori_loop(0, NODES - 2 - node, backward, 0)
            for sub in range(SUBS):
                @pl.when(node < NODES - 1)
                def _():
                    collect(node + 1, h, sub)

                @pl.when(node > blocks[h])
                def _():
                    spread(node - 1, h, sub)

    @pl.when(blocks[0] < first)
    def _():
        v_copy().start()

    for h in (0, 1):
        def remaining(i, carry):
            spread(node - 2 - i, h, None)
            return carry

        lax.fori_loop(0, node - 1 - jnp.maximum(blocks[h], first), remaining, 0)

    for h in range(2):
        scaled[h] = zacc[h] * weights[h]

    kept, sent = upper, 1 - upper

    def x_copy():
        target = device(node, mirror, share)
        return remote(scaled.at[sent], xrecv, x_send, x_recv, target)

    def a_copy(h):
        target = device(node, node, share)
        return remote(scaled.at[h], across.at[blocks[h], upper], a_send.at[h], a_recv.at[blocks[h], upper], target)

    def t_copy(k, half, s):
        columns = pl.ds(s * ROWS, ROWS)
        return remote(
            across.at[k, half, slice(None), columns], trecv.at[share, half],
            t_send.at[k, half, s], t_recv.at[share, half], device(k, plane, s),
        )

    def d_copy(h, s):
        return remote(
            scaled.at[h, slice(None), pl.ds(s * ROWS, ROWS)], trecv.at[share, upper],
            t_send.at[blocks[h], upper, s], t_recv.at[share, upper], device(blocks[h], node, s),
        )

    def arrival(s, half):
        tile = trecv.at[s, half]
        return remote(tile, tile, t_send.at[0, 0, 0], t_recv.at[s, half], device(plane, plane, s))

    @pl.when(node >= mirror)
    def _():
        x_copy().start()

    for h in range(2):
        @pl.when(jnp.logical_and(node > blocks[h], node <= DIRECT))
        def _():
            for s in range(SHARES):
                d_copy(h, s).start()

        @pl.when(jnp.logical_and(node > jnp.maximum(blocks[h], DIRECT), node != plane))
        def _():
            a_copy(h).start()

        @pl.when(jnp.logical_and(node > jnp.maximum(blocks[h], DIRECT), node == plane))
        def _():
            across[blocks[h], upper] = scaled[h]

    @pl.when(node >= plane)
    def _():
        out_ref[pl.ds(upper * HALF, HALF)] = scaled[kept]
        x_copy().wait_recv()
        out_ref[pl.ds((1 - upper) * HALF, HALF)] = xrecv[...]

    @pl.when(jnp.logical_and(node == plane, node > DIRECT))
    def _():
        def deal(i, carry):
            k = node - 1 - i
            for half in range(2):
                source = jnp.minimum(k, NODES - 1 - k) if half == 0 else jnp.maximum(k, NODES - 1 - k)

                @pl.when(source != plane)
                def _():
                    into = across.at[k, half]
                    remote(into, into, a_send.at[0], a_recv.at[k, half], device(node, source, share)).wait_recv()

                for s in range(SHARES):
                    t_copy(k, half, s).start()
            return carry

        lax.fori_loop(0, node, deal, 0)

    @pl.when(node < plane)
    def _():
        for s in range(SHARES):
            for half in range(2):
                arrival(s, half).wait_recv()
            tiles = jnp.concatenate([trecv[s, 0], trecv[s, 1]], 0)
            out_ref[:, s * ROWS : (s + 1) * ROWS] = tiles.T

    @pl.when(node >= mirror)
    def _():
        x_copy().wait_send()

    @pl.when(jnp.logical_and(node == plane, node > DIRECT))
    def _():
        def drain_t(k, carry):
            for half in range(2):
                for s in range(SHARES):
                    t_copy(k, half, s).wait_send()
            return carry

        lax.fori_loop(0, node, drain_t, 0)

    for kind in range(2):
        for distance in range(AHEAD + 1):
            def drained(k, slot, sub):
                y_copy(slot, sub).wait_send()
                c_copy(slot, sub, 0).wait_send()
                c_copy(slot, sub, 1).wait_send()

            each(distance, kind, drained)
            for sub in range(SUBS):
                sends(distance, sub, kind, lambda k, slot, i, way: z_copy(slot, i, way).wait_send())

    @pl.when(plane < first)
    def _():
        hand_over().wait_send()

    @pl.when(blocks[0] < first)
    def _():
        v_copy().wait_send()

    @pl.when(jnp.logical_and(node > blocks[0], jnp.logical_and(node >= 1, node <= NODES - 2 - KEPT)))
    def _():
        m_copy(node, 0, 0, None).wait_send()

    @pl.when(blocks[0] < helped)
    def _():
        s_copy().wait_send()

        def drain_early(to, carry):
            @pl.when(to != node)
            def _():
                early_copy(to).wait_send()

            return carry

        lax.fori_loop(blocks[0], helped, drain_early, 0)

    for h in range(2):
        @pl.when(node > blocks[h])
        def _():
            @pl.when(jnp.logical_and(node != plane, node > DIRECT))
            def _():
                a_copy(h).wait_send()

            @pl.when(node <= DIRECT)
            def _():
                for s in range(SHARES):
                    d_copy(h, s).wait_send()

            for sub in range(SUBS):
                p_copy(node, node - 1, h, sub).wait_send()

                @pl.when(node < NODES - 1)
                def _():
                    m_copy(node, node + 1, h, sub).wait_send()

        def drain_m(target, carry):
            m_copy(node, target, h, None).wait_send()
            return carry

        def drain_p(target, carry):
            p_copy(node, target, h, None).wait_send()
            return carry

        reach = jnp.minimum(node + KEPT + 1, NODES)
        lax.fori_loop(node + 2, jnp.where(node > blocks[h], reach, 0), drain_m, 0)
        lax.fori_loop(jnp.maximum(blocks[h], first), node - 1, drain_p, 0)


def shards(factor_panels, diag_inverse, block_lists, parent):
    f32, bf16, i32 = jnp.float32, jnp.bfloat16, jnp.int32
    dma = pltpu.SemaphoreType.DMA
    anywhere = pl.BlockSpec(memory_space=pl.ANY)
    messages = pltpu.VMEM((NODES, 2, HALF, WIDTH), f32)
    pair = pltpu.VMEM((2, HALF, WIDTH), f32)
    half = pltpu.VMEM((HALF, WIDTH), f32)
    row = pltpu.VMEM((NODES, WIDTH, WIDTH), bf16)
    block = pltpu.VMEM((WIDTH, WIDTH), bf16)
    flags = dma((NODES, 2, 2))
    inverse = pl.pallas_call(
        kernel,
        out_shape=jax.ShapeDtypeStruct((ROWS, WIDTH), f32),
        in_specs=[anywhere] * 4,
        out_specs=pl.BlockSpec(memory_space=pltpu.VMEM),
        scratch_shapes=[
            pltpu.VMEM((ROWS, WIDTH), f32), pltpu.VMEM((WIDTH, WIDTH), f32),
            pltpu.SMEM((NODES, NODES - 1), i32), pltpu.SMEM((NODES,), i32),
            pltpu.VMEM((NODES, SHARES, ROWS, WIDTH), f32),
            row, row, block, block, pair, messages, pair, messages, messages, half,
            messages, pltpu.VMEM((SHARES, 2, HALF, ROWS), f32),
            pair, half, half, half,
            dma((4,)), flags, dma((NODES, SUBS)), dma((NODES, SUBS)), dma((NODES, SUBS)),
            flags, flags, *[dma(())] * 6,
            flags, flags, flags, flags, dma(()), dma(()), dma((2,)), dma((NODES, 2)),
            dma((NODES, 2, SHARES)), dma((SHARES, 2)),
        ],
        compiler_params=pltpu.CompilerParams(
            collective_id=0, has_side_effects=True, vmem_limit_bytes=60 * 2**20
        ),
        name="selected_inverse",
    )(factor_panels[0], diag_inverse[0], block_lists, parent)
    return inverse[None]


def solution(mesh):
    placed = (P("prow", "pcol", None), P("prow", None, None), P(), P())
    return jax.shard_map(
        shards, mesh=mesh, in_specs=placed, out_specs=P("prow", "pcol", None), check_vma=False
    )
```

```python
import jax
import jax.numpy as jnp
from jax import lax
from jax.experimental import pallas as pl
from jax.experimental.pallas import tpu as pltpu
from jax.sharding import PartitionSpec as P

MESH = pl.DeviceIdType.MESH
NODES = 8
WIDTH = 512
SHARES = 4
ROWS = 128
HALF = ROWS // 2
SUBS = 2
CUTS = 2
PIECE = HALF // SUBS
DIRECT = 3
AHEAD, BEHIND = 4, 3
KEPT = 5
RELAY, PREPARE = 1, 2


def pattern_weight(lists_ref, parent_ref, target, node):
    found = parent_ref[target] == node
    for i in range(NODES - 1):
        found = jnp.logical_or(found, lists_ref[target, i] == node)
    return jnp.where(found, 1.0, 0.0).astype(jnp.float32)


def split(value):
    high = value.astype(jnp.bfloat16)
    low = (value - high.astype(jnp.float32)).astype(jnp.bfloat16)
    return high, low


def product(left, high_ref, low_ref, transposed):
    high, low = split(left)
    dims = (((1,), (1 if transposed else 0,)), ((), ()))
    rows = left.shape[0]
    both = lax.dot_general(
        jnp.concatenate([high, low], 0), high_ref[...], dims, preferred_element_type=jnp.float32
    )
    cross = lax.dot_general(high, low_ref[...], dims, preferred_element_type=jnp.float32)
    return both[:rows] + both[rows:] + cross


def kernel(
    f_hbm, d_hbm, lists_hbm, parent_hbm, out_ref,
    f_ref, d_ref, lists_ref, parent_ref,
    raw, lhi, llo, dhi, dlo, mine, mrecv, zacc, psend, precv, xrecv, across, trecv,
    scaled, part_sum, part_recv, solved,
    in_sem, z_send, z_recv, y_send, y_recv, c_send, c_recv,
    h_send, h_recv, s_send, s_recv, v_send, v_recv,
    m_send, m_recv, p_send, p_recv, x_send, x_recv, a_send, a_recv, t_send, t_recv,
):
    node = lax.axis_index("prow")
    col = lax.axis_index("pcol")
    plane = col // SHARES
    share = lax.rem(col, SHARES)
    y_low, core = share // 2, lax.rem(share, 2)
    y_share = (1 - y_low) * 2 + core
    c_share = y_low * 2 + 1 - core
    upper = plane // (NODES // 2)
    mirror = NODES - 1 - plane
    blocks = (jnp.minimum(plane, mirror), jnp.maximum(plane, mirror))
    first = jnp.maximum(node - KEPT, 0)
    friend = NODES - 1 - node
    helped = NODES - 1 - KEPT - node

    def device(n, z, s):
        return (n, z * SHARES + s)

    barrier = pltpu.get_barrier_semaphore()

    def greet(target):
        pl.semaphore_signal(barrier, device_id=target, device_id_type=MESH)

    for step in range(1, NODES):
        greet(device(lax.rem(node + step, NODES), plane, share))
    greet(device(node, lax.rem(plane + 1, NODES), share))
    greet(device(node, lax.rem(plane + NODES - 1, NODES), share))
    greet(device(node, mirror, share))
    greet(device(node, plane, y_share))
    greet(device(node, plane, c_share))

    @pl.when(node < plane)
    def _():
        @pl.when(plane > DIRECT)
        def _():
            for s in range(SHARES):
                greet(device(plane, plane, s))

        @pl.when(plane <= DIRECT)
        def _():
            for s in range(SHARES):
                greet(device(plane, node, s))
                greet(device(plane, NODES - 1 - node, s))

    @pl.when(jnp.logical_and(node == plane, node > DIRECT))
    def _():
        for step in range(1, NODES):
            greet(device(node, lax.rem(plane + step, NODES), share))


    loads = [
        pltpu.make_async_copy(src, dst, in_sem.at[i])
        for i, (src, dst) in enumerate(
            [(lists_hbm, lists_ref), (parent_hbm, parent_ref), (f_hbm, f_ref), (d_hbm, d_ref)]
        )
    ]
    for load in loads:
        load.start()
    for load in loads[:3]:
        load.wait()

    @pl.when(plane < node)
    def _():
        raw[plane, share] = f_ref[...] * pattern_weight(lists_ref, parent_ref, plane, node)

    for h in range(2):
        offset = share * ROWS + upper * HALF
        rows = lax.broadcasted_iota(jnp.int32, (HALF, WIDTH), 0) + offset
        columns = lax.broadcasted_iota(jnp.int32, (HALF, WIDTH), 1)
        unit = jnp.where(rows == columns, 1.0, 0.0).astype(jnp.float32)
        here = jnp.where(node == blocks[h], 1.0, 0.0).astype(jnp.float32)
        mrecv[blocks[h], h] = unit
        mine[h] = unit * here
    weights = []
    for h in range(2):
        weight = pattern_weight(lists_ref, parent_ref, blocks[h], node)
        weights.append(jnp.where(node == blocks[h], 1.0, weight))
    loads[3].wait()
    high, low = split(d_ref[...])
    dhi[...] = high
    dlo[...] = low
    relayed = jnp.where(node == plane, SHARES * node, 1)
    direct = SHARES * sum(jnp.where(node > blocks[h], 1, 0) for h in range(2))
    greeted = NODES - 1 + 5 + jnp.where(node > DIRECT, relayed, direct)
    pl.semaphore_wait(barrier, greeted)

    def remote(src, dst, send, recv, target):
        return pltpu.make_async_remote_copy(
            src_ref=src, dst_ref=dst, send_sem=send, recv_sem=recv,
            device_id=target, device_id_type=MESH,
        )

    def z_copy(k, sub, way):
        step = 1 if way == 0 else NODES - 1
        here = raw.at[k, share, pl.ds(sub * HALF, HALF)]
        target = device(node, lax.rem(plane + step, NODES), share)
        return remote(here, here, z_send.at[k, sub, way], z_recv.at[k, sub], target)

    def y_copy(k, sub):
        here = raw.at[k, share, pl.ds(sub * HALF, HALF)]
        target = device(node, plane, y_share)
        return remote(here, here, y_send.at[k, sub], y_recv.at[k, sub], target)

    def c_copy(k, sub, which):
        here = raw.at[k, share if which == 0 else y_share, pl.ds(sub * HALF, HALF)]
        target = device(node, plane, c_share)
        return remote(here, here, c_send.at[k, sub, which], c_recv.at[k, sub, which], target)

    def part(ref, index, h, sub):
        if sub is None:
            return ref.at[index, h] if index is not None else ref.at[h]
        rows = pl.ds(sub * PIECE, PIECE)
        return ref.at[index, h, rows] if index is not None else ref.at[h, rows]

    def m_copy(k, target, h, sub):
        i = sub or 0
        return remote(
            part(mine, None, h, sub), part(mrecv, k, h, sub),
            m_send.at[target, h, i], m_recv.at[k, h, i], device(target, plane, share),
        )

    def p_copy(k, target, h, sub):
        i = sub or 0
        return remote(
            part(psend, target, h, sub), part(precv, k, h, sub),
            p_send.at[target, h, i], p_recv.at[k, h, i], device(target, plane, share),
        )

    def member(k, kind):
        return k < helped if kind else jnp.logical_and(k >= first, k < node)

    def used(k, kind):
        return jnp.logical_and(member(k, kind), k >= blocks[0])

    def passes(k, way, distance, kind):
        if distance > (BEHIND if way else AHEAD):
            return False
        if way == 0:
            return jnp.logical_and(member(k, kind), k >= 2)
        return jnp.logical_and(member(k, kind), jnp.logical_or(k >= 1, distance <= 1))

    def ring(distance):
        ways = [0, 1] if distance else [0]
        return [(way, lax.rem(plane + (distance if way else NODES - distance), NODES)) for way in ways]

    def each(distance, kind, action):
        for way, k in ring(distance):
            if distance == 0 or passes(k, way, distance, kind) is not False:
                @pl.when(used(k, kind))
                def _():
                    for sub in range(CUTS):
                        action(k, k + KEPT * kind, sub)

    def sends(distance, sub, kind, action):
        for way, k in ring(distance):
            for onward in ([0, 1] if distance == 0 else [way]):
                further = passes(k, onward, distance + 1, kind)
                if further is not False:
                    @pl.when(further)
                    def _():
                        action(k, k + KEPT * kind, sub, onward)

    def land(distance, kind):
        for sub in range(CUTS):
            for way, k in ring(distance):
                arrives = passes(k, way, distance, kind) if distance else False
                if arrives is not False:
                    @pl.when(arrives)
                    def _():
                        z_copy(k + KEPT * kind, sub, way).wait_recv()

            sends(distance, sub, kind, lambda k, slot, i, way: z_copy(slot, i, way).start())
            for way, k in ring(distance):
                if distance == 0 or passes(k, way, distance, kind) is not False:
                    @pl.when(used(k, kind))
                    def _():
                        y_copy(k + KEPT * kind, sub).start()
                        c_copy(k + KEPT * kind, sub, 0).start()

    def relay(distance, kind):
        def action(k, slot, sub):
            y_copy(slot, sub).wait_recv()
            c_copy(slot, sub, 1).start()

        each(distance, kind, action)

    def prepare(k, slot, sub):
        c_copy(slot, sub, 0).wait_recv()
        c_copy(slot, sub, 1).wait_recv()
        for i in range(SHARES):
            high, low = split(raw[slot, i, sub * HALF : (sub + 1) * HALF])
            rows = slice(i * ROWS + sub * HALF, i * ROWS + (sub + 1) * HALF)
            lhi[slot, rows] = high
            llo[slot, rows] = low

    def gather(kind):
        for step in range(AHEAD + 1 + PREPARE):
            if step <= AHEAD:
                land(step, kind)
            if 0 <= step - RELAY <= AHEAD:
                relay(step - RELAY, kind)
            if 0 <= step - PREPARE <= AHEAD:
                each(step - PREPARE, kind, prepare)

    def hand_over():
        target = device(friend, plane, share)
        return remote(raw.at[plane, share], raw.at[plane + KEPT, share], h_send, h_recv, target)

    @pl.when(plane < first)
    def _():
        hand_over().start()

    gather(0)

    def forward(k, carry):
        for h in range(2):
            @pl.when(k >= blocks[h])
            def _():
                @pl.when(k > blocks[h])
                def _():
                    m_copy(k, node, h, None).wait_recv()

                mine[h] = mine[h] - product(mrecv[k, h], lhi.at[k], llo.at[k], True)

        return carry

    lax.fori_loop(first, node - 1, forward, 0)

    def s_copy():
        return remote(part_sum, part_recv, s_send, s_recv, device(friend, plane, share))

    @pl.when(blocks[0] < first)
    def _():
        s_copy().wait_recv()
        mine[0] = mine[0] - part_recv[...]

    for h in range(2):
        @pl.when(node > blocks[h])
        def _():
            last = node - 1
            for sub in range(SUBS):
                @pl.when(last > blocks[h])
                def _():
                    m_copy(last, node, h, sub).wait_recv()

                rows = slice(sub * PIECE, (sub + 1) * PIECE)
                mine[h, rows] = mine[h, rows] - product(
                    mrecv[last, h, rows], lhi.at[last], llo.at[last], True
                )

                @pl.when(node < NODES - 1)
                def _():
                    m_copy(node, node + 1, h, sub).start()

            def body(target, carry):
                m_copy(node, target, h, None).start()
                return carry

            lax.fori_loop(node + 2, jnp.minimum(node + KEPT + 1, NODES), body, 0)

    @pl.when(jnp.logical_and(node > blocks[0], jnp.logical_and(node >= 1, node <= NODES - 2 - KEPT)))
    def _():
        m_copy(node, 0, 0, None).start()
        mrecv[node, 0] = mine[0]

    @pl.when(plane < helped)
    def _():
        remote(raw.at[0, 0], raw.at[0, 0], h_send, h_recv, device(friend, plane, share)).wait_recv()

    gather(1)

    @pl.when(blocks[0] < helped)
    def _():
        part_sum[...] = jnp.zeros_like(part_sum)

        def term(k, carry):
            @pl.when(jnp.logical_and(k > blocks[0], k != node))
            def _():
                m_copy(k, node, 0, None).wait_recv()

            part_sum[...] += product(mrecv[k, 0], lhi.at[k + KEPT], llo.at[k + KEPT], True)
            return carry

        lax.fori_loop(blocks[0], helped, term, 0)
        s_copy().start()

    def v_copy():
        return remote(zacc.at[0], solved, v_send, v_recv, device(friend, plane, share))

    def early_copy(to):
        return remote(
            psend.at[to + KEPT, 0], precv.at[friend, 0],
            p_send.at[to + KEPT, 0, 0], p_recv.at[friend, 0, 0], device(to, plane, share),
        )

    @pl.when(blocks[0] < helped)
    def _():
        v_copy().wait_recv()

        def early(to, carry):
            psend[to + KEPT, 0] = product(solved[...], lhi.at[to + KEPT], llo.at[to + KEPT], False)

            @pl.when(to != node)
            def _():
                early_copy(to).start()

            @pl.when(to == node)
            def _():
                precv[friend, 0] = psend[to + KEPT, 0]

            return carry

        lax.fori_loop(blocks[0], helped, early, 0)

    def collect(k, h, sub):
        if h == 0 and sub is None:
            @pl.when(jnp.logical_not(jnp.logical_and(k == friend, node < helped)))
            def _():
                p_copy(k, node, h, sub).wait_recv()
        else:
            p_copy(k, node, h, sub).wait_recv()
        rows = slice(0, HALF) if sub is None else slice(sub * PIECE, (sub + 1) * PIECE)
        zacc[h, rows] = zacc[h, rows] - precv[k, h, rows]

    def spread(to, h, sub):
        rows = slice(0, HALF) if sub is None else slice(sub * PIECE, (sub + 1) * PIECE)
        psend[to, h, rows] = product(zacc[h, rows], lhi.at[to], llo.at[to], False)
        p_copy(node, to, h, sub).start()

    for h in (0, 1):
        @pl.when(node >= blocks[h])
        def _():
            zacc[h] = product(mine[h], dhi, dlo, False)

            def backward(i, carry):
                collect(NODES - 1 - i, h, None)
                return carry

            lax.fori_loop(0, NODES - 2 - node, backward, 0)
            for sub in range(SUBS):
                @pl.when(node < NODES - 1)
                def _():
                    collect(node + 1, h, sub)

                @pl.when(node > blocks[h])
                def _():
                    spread(node - 1, h, sub)

    @pl.when(blocks[0] < first)
    def _():
        v_copy().start()

    for h in (0, 1):
        def remaining(i, carry):
            spread(node - 2 - i, h, None)
            return carry

        lax.fori_loop(0, node - 1 - jnp.maximum(blocks[h], first), remaining, 0)

    for h in range(2):
        scaled[h] = jnp.where(weights[h] > 0.0, zacc[h], 0.0)

    kept, sent = upper, 1 - upper

    def x_copy():
        target = device(node, mirror, share)
        return remote(scaled.at[sent], xrecv, x_send, x_recv, target)

    def a_copy(h):
        target = device(node, node, share)
        return remote(scaled.at[h], across.at[blocks[h], upper], a_send.at[h], a_recv.at[blocks[h], upper], target)

    def t_copy(k, half, s):
        columns = pl.ds(s * ROWS, ROWS)
        return remote(
            across.at[k, half, slice(None), columns], trecv.at[share, half],
            t_send.at[k, half, s], t_recv.at[share, half], device(k, plane, s),
        )

    def d_copy(h, s):
        return remote(
            scaled.at[h, slice(None), pl.ds(s * ROWS, ROWS)], trecv.at[share, upper],
            t_send.at[blocks[h], upper, s], t_recv.at[share, upper], device(blocks[h], node, s),
        )

    def arrival(s, half):
        tile = trecv.at[s, half]
        return remote(tile, tile, t_send.at[0, 0, 0], t_recv.at[s, half], device(plane, plane, s))

    @pl.when(node >= mirror)
    def _():
        x_copy().start()

    for h in range(2):
        @pl.when(jnp.logical_and(node > blocks[h], node <= DIRECT))
        def _():
            for s in range(SHARES):
                d_copy(h, s).start()

        @pl.when(jnp.logical_and(node > jnp.maximum(blocks[h], DIRECT), node != plane))
        def _():
            a_copy(h).start()

        @pl.when(jnp.logical_and(node > jnp.maximum(blocks[h], DIRECT), node == plane))
        def _():
            across[blocks[h], upper] = scaled[h]

    @pl.when(node >= plane)
    def _():
        out_ref[pl.ds(upper * HALF, HALF)] = scaled[kept]
        x_copy().wait_recv()
        out_ref[pl.ds((1 - upper) * HALF, HALF)] = xrecv[...]

    @pl.when(jnp.logical_and(node == plane, node > DIRECT))
    def _():
        def deal(i, carry):
            k = node - 1 - i
            for half in range(2):
                source = jnp.minimum(k, NODES - 1 - k) if half == 0 else jnp.maximum(k, NODES - 1 - k)

                @pl.when(source != plane)
                def _():
                    into = across.at[k, half]
                    remote(into, into, a_send.at[0], a_recv.at[k, half], device(node, source, share)).wait_recv()

                for s in range(SHARES):
                    t_copy(k, half, s).start()
            return carry

        lax.fori_loop(0, node, deal, 0)

    @pl.when(node < plane)
    def _():
        for s in range(SHARES):
            for half in range(2):
                arrival(s, half).wait_recv()
            tiles = jnp.concatenate([trecv[s, 0], trecv[s, 1]], 0)
            out_ref[:, s * ROWS : (s + 1) * ROWS] = tiles.T

    @pl.when(node >= mirror)
    def _():
        x_copy().wait_send()

    @pl.when(jnp.logical_and(node == plane, node > DIRECT))
    def _():
        def drain_t(k, carry):
            for half in range(2):
                for s in range(SHARES):
                    t_copy(k, half, s).wait_send()
            return carry

        lax.fori_loop(0, node, drain_t, 0)

    for kind in range(2):
        for distance in range(AHEAD + 1):
            def drained(k, slot, sub):
                y_copy(slot, sub).wait_send()
                c_copy(slot, sub, 0).wait_send()
                c_copy(slot, sub, 1).wait_send()

            each(distance, kind, drained)
            for sub in range(CUTS):
                sends(distance, sub, kind, lambda k, slot, i, way: z_copy(slot, i, way).wait_send())

    @pl.when(plane < first)
    def _():
        hand_over().wait_send()

    @pl.when(blocks[0] < first)
    def _():
        v_copy().wait_send()

    @pl.when(jnp.logical_and(node > blocks[0], jnp.logical_and(node >= 1, node <= NODES - 2 - KEPT)))
    def _():
        m_copy(node, 0, 0, None).wait_send()

    @pl.when(blocks[0] < helped)
    def _():
        s_copy().wait_send()

        def drain_early(to, carry):
            @pl.when(to != node)
            def _():
                early_copy(to).wait_send()

            return carry

        lax.fori_loop(blocks[0], helped, drain_early, 0)

    for h in range(2):
        @pl.when(node > blocks[h])
        def _():
            @pl.when(jnp.logical_and(node != plane, node > DIRECT))
            def _():
                a_copy(h).wait_send()

            @pl.when(node <= DIRECT)
            def _():
                for s in range(SHARES):
                    d_copy(h, s).wait_send()

            for sub in range(SUBS):
                p_copy(node, node - 1, h, sub).wait_send()

                @pl.when(node < NODES - 1)
                def _():
                    m_copy(node, node + 1, h, sub).wait_send()

        def drain_m(target, carry):
            m_copy(node, target, h, None).wait_send()
            return carry

        def drain_p(target, carry):
            p_copy(node, target, h, None).wait_send()
            return carry

        reach = jnp.minimum(node + KEPT + 1, NODES)
        lax.fori_loop(node + 2, jnp.where(node > blocks[h], reach, 0), drain_m, 0)
        lax.fori_loop(jnp.maximum(blocks[h], first), node - 1, drain_p, 0)


def shards(factor_panels, diag_inverse, block_lists, parent):
    f32, bf16, i32 = jnp.float32, jnp.bfloat16, jnp.int32
    dma = pltpu.SemaphoreType.DMA
    anywhere = pl.BlockSpec(memory_space=pl.ANY)
    messages = pltpu.VMEM((NODES, 2, HALF, WIDTH), f32)
    pair = pltpu.VMEM((2, HALF, WIDTH), f32)
    half = pltpu.VMEM((HALF, WIDTH), f32)
    row = pltpu.VMEM((NODES, WIDTH, WIDTH), bf16)
    block = pltpu.VMEM((WIDTH, WIDTH), bf16)
    flags = dma((NODES, 2, SUBS))
    row_cuts, cuts = dma((NODES, CUTS)), dma((NODES, CUTS, 2))
    inverse = pl.pallas_call(
        kernel,
        out_shape=jax.ShapeDtypeStruct((ROWS, WIDTH), f32),
        in_specs=[anywhere] * 4,
        out_specs=pl.BlockSpec(memory_space=pltpu.VMEM),
        scratch_shapes=[
            pltpu.VMEM((ROWS, WIDTH), f32), pltpu.VMEM((WIDTH, WIDTH), f32),
            pltpu.SMEM((NODES, NODES - 1), i32), pltpu.SMEM((NODES,), i32),
            pltpu.VMEM((NODES, SHARES, ROWS, WIDTH), f32),
            row, row, block, block, pair, messages, pair, messages, messages, half,
            messages, pltpu.VMEM((SHARES, 2, HALF, ROWS), f32),
            pair, half, half, half,
            dma((4,)), cuts, row_cuts, row_cuts, row_cuts, cuts, cuts, *[dma(())] * 6,
            flags, flags, flags, flags, dma(()), dma(()), dma((2,)), dma((NODES, 2)),
            dma((NODES, 2, SHARES)), dma((SHARES, 2)),
        ],
        compiler_params=pltpu.CompilerParams(
            collective_id=0, has_side_effects=True, vmem_limit_bytes=60 * 2**20
        ),
        name="selected_inverse",
    )(factor_panels[0], diag_inverse[0], block_lists, parent)
    return inverse[None]


def solution(mesh):
    placed = (P("prow", "pcol", None), P("prow", None, None), P(), P())
    return jax.shard_map(
        shards, mesh=mesh, in_specs=placed, out_specs=P("prow", "pcol", None), check_vma=False
    )
```

```python
import jax
import jax.numpy as jnp
from jax import lax
from jax.experimental import pallas as pl
from jax.experimental.pallas import tpu as pltpu
from jax.sharding import PartitionSpec as P

MESH = pl.DeviceIdType.MESH
NODES = 8
WIDTH = 512
SHARES = 4
ROWS = 128
HALF = ROWS // 2
SUBS = 2
CUTS = 2
PIECE = HALF // SUBS
DIRECT = 3
AHEAD, BEHIND = 4, 3
KEPT = 5
RELAY, PREPARE = 1, 2


def pattern_weight(lists_ref, parent_ref, target, node):
    found = parent_ref[target] == node
    for i in range(NODES - 1):
        found = jnp.logical_or(found, lists_ref[target, i] == node)
    return jnp.where(found, 1.0, 0.0).astype(jnp.float32)


def split(value):
    high = value.astype(jnp.bfloat16)
    low = (value - high.astype(jnp.float32)).astype(jnp.bfloat16)
    return high, low


def product(left, high_ref, low_ref, transposed):
    high, low = split(left)
    dims = (((1,), (1 if transposed else 0,)), ((), ()))
    rows = left.shape[0]
    both = lax.dot_general(
        jnp.concatenate([high, low], 0), high_ref[...], dims, preferred_element_type=jnp.float32
    )
    cross = lax.dot_general(high, low_ref[...], dims, preferred_element_type=jnp.float32)
    return both[:rows] + both[rows:] + cross


def kernel(
    f_hbm, d_hbm, lists_hbm, parent_hbm, out_ref,
    f_ref, d_ref, lists_ref, parent_ref,
    raw, lhi, llo, dhi, dlo, mine, mrecv, zacc, psend, precv, xrecv, across, trecv,
    scaled, part_sum, part_recv, solved,
    in_sem, z_send, z_recv, y_send, y_recv, c_send, c_recv,
    h_send, h_recv, s_send, s_recv, v_send, v_recv,
    m_send, m_recv, p_send, p_recv, x_send, x_recv, a_send, a_recv, t_send, t_recv,
):
    node = lax.axis_index("prow")
    col = lax.axis_index("pcol")
    plane = col // SHARES
    share = lax.rem(col, SHARES)
    y_low, core = share // 2, lax.rem(share, 2)
    y_share = (1 - y_low) * 2 + core
    c_share = y_low * 2 + 1 - core
    upper = plane // (NODES // 2)
    mirror = NODES - 1 - plane
    blocks = (jnp.minimum(plane, mirror), jnp.maximum(plane, mirror))
    first = jnp.maximum(node - KEPT, 0)
    friend = NODES - 1 - node
    helped = NODES - 1 - KEPT - node

    def device(n, z, s):
        return (n, z * SHARES + s)

    barrier = pltpu.get_barrier_semaphore()

    def greet(target):
        pl.semaphore_signal(barrier, device_id=target, device_id_type=MESH)

    for step in range(1, NODES):
        greet(device(lax.rem(node + step, NODES), plane, share))
    greet(device(node, lax.rem(plane + 1, NODES), share))
    greet(device(node, lax.rem(plane + NODES - 1, NODES), share))
    greet(device(node, mirror, share))
    greet(device(node, plane, y_share))
    greet(device(node, plane, c_share))

    @pl.when(node < plane)
    def _():
        @pl.when(plane > DIRECT)
        def _():
            for s in range(SHARES):
                greet(device(plane, plane, s))

        @pl.when(plane <= DIRECT)
        def _():
            for s in range(SHARES):
                greet(device(plane, node, s))
                greet(device(plane, NODES - 1 - node, s))

    @pl.when(jnp.logical_and(node == plane, node > DIRECT))
    def _():
        for step in range(1, NODES):
            greet(device(node, lax.rem(plane + step, NODES), share))


    @pl.when(plane < helped)
    def _():
        greet(device(friend, plane, y_share))

    loads = [
        pltpu.make_async_copy(src, dst, in_sem.at[i])
        for i, (src, dst) in enumerate(
            [(lists_hbm, lists_ref), (parent_hbm, parent_ref), (f_hbm, f_ref), (d_hbm, d_ref)]
        )
    ]
    for load in loads:
        load.start()
    for load in loads[:3]:
        load.wait()

    @pl.when(plane < node)
    def _():
        raw[plane, share] = f_ref[...] * pattern_weight(lists_ref, parent_ref, plane, node)

    for h in range(2):
        offset = share * ROWS + upper * HALF
        rows = lax.broadcasted_iota(jnp.int32, (HALF, WIDTH), 0) + offset
        columns = lax.broadcasted_iota(jnp.int32, (HALF, WIDTH), 1)
        unit = jnp.where(rows == columns, 1.0, 0.0).astype(jnp.float32)
        here = jnp.where(node == blocks[h], 1.0, 0.0).astype(jnp.float32)
        mrecv[blocks[h], h] = unit
        mine[h] = unit * here
    weights = []
    for h in range(2):
        weight = pattern_weight(lists_ref, parent_ref, blocks[h], node)
        weights.append(jnp.where(node == blocks[h], 1.0, weight))
    loads[3].wait()
    high, low = split(d_ref[...])
    dhi[...] = high
    dlo[...] = low
    relayed = jnp.where(node == plane, SHARES * node, 1)
    direct = SHARES * sum(jnp.where(node > blocks[h], 1, 0) for h in range(2))
    greeted = NODES - 1 + 5 + jnp.where(node > DIRECT, relayed, direct) + jnp.where(plane < first, 1, 0)
    pl.semaphore_wait(barrier, greeted)

    def remote(src, dst, send, recv, target):
        return pltpu.make_async_remote_copy(
            src_ref=src, dst_ref=dst, send_sem=send, recv_sem=recv,
            device_id=target, device_id_type=MESH,
        )

    def z_copy(k, sub, way, kind):
        step = 1 if way == 0 else NODES - 1
        here = raw.at[k, y_share if kind else share, pl.ds(sub * HALF, HALF)]
        target = device(node, lax.rem(plane + step, NODES), share)
        return remote(here, here, z_send.at[k, sub, way], z_recv.at[k, sub], target)

    def y_copy(k, sub, kind):
        here = raw.at[k, y_share if kind else share, pl.ds(sub * HALF, HALF)]
        target = device(node, plane, y_share)
        return remote(here, here, y_send.at[k, sub], y_recv.at[k, sub], target)

    def c_copy(k, sub, which, kind):
        here = raw.at[k, share if which == kind else y_share, pl.ds(sub * HALF, HALF)]
        target = device(node, plane, c_share)
        return remote(here, here, c_send.at[k, sub, which], c_recv.at[k, sub, which], target)

    def part(ref, index, h, sub):
        if sub is None:
            return ref.at[index, h] if index is not None else ref.at[h]
        rows = pl.ds(sub * PIECE, PIECE)
        return ref.at[index, h, rows] if index is not None else ref.at[h, rows]

    def m_copy(k, target, h, sub):
        i = sub or 0
        return remote(
            part(mine, None, h, sub), part(mrecv, k, h, sub),
            m_send.at[target, h, i], m_recv.at[k, h, i], device(target, plane, share),
        )

    def p_copy(k, target, h, sub):
        i = sub or 0
        return remote(
            part(psend, target, h, sub), part(precv, k, h, sub),
            p_send.at[target, h, i], p_recv.at[k, h, i], device(target, plane, share),
        )

    def member(k, kind):
        return k < helped if kind else jnp.logical_and(k >= first, k < node)

    def used(k, kind):
        return jnp.logical_and(member(k, kind), k >= blocks[0])

    def passes(k, way, distance, kind):
        if distance > (BEHIND if way else AHEAD):
            return False
        if way == 0:
            return jnp.logical_and(member(k, kind), k >= 2)
        return jnp.logical_and(member(k, kind), jnp.logical_or(k >= 1, distance <= 1))

    def ring(distance):
        ways = [0, 1] if distance else [0]
        return [(way, lax.rem(plane + (distance if way else NODES - distance), NODES)) for way in ways]

    def each(distance, kind, action):
        for way, k in ring(distance):
            if distance == 0 or passes(k, way, distance, kind) is not False:
                @pl.when(used(k, kind))
                def _():
                    for sub in range(CUTS):
                        action(k, k + KEPT * kind, sub)

    def sends(distance, sub, kind, action):
        for way, k in ring(distance):
            for onward in ([0, 1] if distance == 0 else [way]):
                further = passes(k, onward, distance + 1, kind)
                if further is not False:
                    @pl.when(further)
                    def _():
                        action(k, k + KEPT * kind, sub, onward)

    def land(distance, kind):
        for sub in range(CUTS):
            for way, k in ring(distance):
                arrives = passes(k, way, distance, kind) if distance else False
                if arrives is not False:
                    @pl.when(arrives)
                    def _():
                        z_copy(k + KEPT * kind, sub, way, kind).wait_recv()

            sends(distance, sub, kind, lambda k, slot, i, way: z_copy(slot, i, way, kind).start())
            for way, k in ring(distance):
                if distance == 0 or passes(k, way, distance, kind) is not False:
                    @pl.when(used(k, kind))
                    def _():
                        y_copy(k + KEPT * kind, sub, kind).start()
                        c_copy(k + KEPT * kind, sub, 0, kind).start()

    def relay(distance, kind):
        def action(k, slot, sub):
            y_copy(slot, sub, kind).wait_recv()
            c_copy(slot, sub, 1, kind).start()

        each(distance, kind, action)

    def prepare(k, slot, sub, kind):
        c_copy(slot, sub, 0, kind).wait_recv()
        c_copy(slot, sub, 1, kind).wait_recv()
        for i in range(SHARES):
            high, low = split(raw[slot, i, sub * HALF : (sub + 1) * HALF])
            rows = slice(i * ROWS + sub * HALF, i * ROWS + (sub + 1) * HALF)
            lhi[slot, rows] = high
            llo[slot, rows] = low

    def gather(kind):
        for step in range(AHEAD + 1 + PREPARE):
            if step <= AHEAD:
                land(step, kind)
            if 0 <= step - RELAY <= AHEAD:
                relay(step - RELAY, kind)
            if 0 <= step - PREPARE <= AHEAD:
                each(step - PREPARE, kind, lambda k, slot, sub: prepare(k, slot, sub, kind))

    def hand_over():
        target = device(friend, plane, y_share)
        return remote(raw.at[plane, share], raw.at[plane + KEPT, share], h_send, h_recv, target)

    @pl.when(plane < first)
    def _():
        hand_over().start()

    gather(0)

    def forward(k, carry):
        for h in range(2):
            @pl.when(k >= blocks[h])
            def _():
                @pl.when(k > blocks[h])
                def _():
                    m_copy(k, node, h, None).wait_recv()

                mine[h] = mine[h] - product(mrecv[k, h], lhi.at[k], llo.at[k], True)

        return carry

    lax.fori_loop(first, node - 1, forward, 0)

    def s_copy():
        return remote(part_sum, part_recv, s_send, s_recv, device(friend, plane, share))

    @pl.when(blocks[0] < first)
    def _():
        s_copy().wait_recv()
        mine[0] = mine[0] - part_recv[...]

    for h in range(2):
        @pl.when(node > blocks[h])
        def _():
            last = node - 1
            for sub in range(SUBS):
                @pl.when(last > blocks[h])
                def _():
                    m_copy(last, node, h, sub).wait_recv()

                rows = slice(sub * PIECE, (sub + 1) * PIECE)
                mine[h, rows] = mine[h, rows] - product(
                    mrecv[last, h, rows], lhi.at[last], llo.at[last], True
                )

                @pl.when(node < NODES - 1)
                def _():
                    m_copy(node, node + 1, h, sub).start()

            def body(target, carry):
                m_copy(node, target, h, None).start()
                return carry

            lax.fori_loop(node + 2, jnp.minimum(node + KEPT + 1, NODES), body, 0)

    @pl.when(jnp.logical_and(node > blocks[0], jnp.logical_and(node >= 1, node <= NODES - 2 - KEPT)))
    def _():
        m_copy(node, 0, 0, None).start()
        mrecv[node, 0] = mine[0]

    @pl.when(plane < helped)
    def _():
        remote(raw.at[0, 0], raw.at[0, 0], h_send, h_recv, device(friend, plane, y_share)).wait_recv()

    gather(1)

    @pl.when(blocks[0] < helped)
    def _():
        part_sum[...] = jnp.zeros_like(part_sum)

        def term(k, carry):
            @pl.when(jnp.logical_and(k > blocks[0], k != node))
            def _():
                m_copy(k, node, 0, None).wait_recv()

            part_sum[...] += product(mrecv[k, 0], lhi.at[k + KEPT], llo.at[k + KEPT], True)
            return carry

        lax.fori_loop(blocks[0], helped, term, 0)
        s_copy().start()

    def v_copy():
        return remote(zacc.at[0], solved, v_send, v_recv, device(friend, plane, share))

    def early_copy(to):
        return remote(
            psend.at[to + KEPT, 0], precv.at[friend, 0],
            p_send.at[to + KEPT, 0, 0], p_recv.at[friend, 0, 0], device(to, plane, share),
        )

    @pl.when(blocks[0] < helped)
    def _():
        v_copy().wait_recv()

        def early(to, carry):
            psend[to + KEPT, 0] = product(solved[...], lhi.at[to + KEPT], llo.at[to + KEPT], False)

            @pl.when(to != node)
            def _():
                early_copy(to).start()

            @pl.when(to == node)
            def _():
                precv[friend, 0] = psend[to + KEPT, 0]

            return carry

        lax.fori_loop(blocks[0], helped, early, 0)

    def collect(k, h, sub):
        if h == 0 and sub is None:
            @pl.when(jnp.logical_not(jnp.logical_and(k == friend, node < helped)))
            def _():
                p_copy(k, node, h, sub).wait_recv()
        else:
            p_copy(k, node, h, sub).wait_recv()
        rows = slice(0, HALF) if sub is None else slice(sub * PIECE, (sub + 1) * PIECE)
        zacc[h, rows] = zacc[h, rows] - precv[k, h, rows]

    def spread(to, h, sub):
        rows = slice(0, HALF) if sub is None else slice(sub * PIECE, (sub + 1) * PIECE)
        psend[to, h, rows] = product(zacc[h, rows], lhi.at[to], llo.at[to], False)
        p_copy(node, to, h, sub).start()

    for h in (0, 1):
        @pl.when(node >= blocks[h])
        def _():
            zacc[h] = product(mine[h], dhi, dlo, False)

            def backward(i, carry):
                collect(NODES - 1 - i, h, None)
                return carry

            lax.fori_loop(0, NODES - 2 - node, backward, 0)
            for sub in range(SUBS):
                @pl.when(node < NODES - 1)
                def _():
                    collect(node + 1, h, sub)

                @pl.when(node > blocks[h])
                def _():
                    spread(node - 1, h, sub)

    @pl.when(blocks[0] < first)
    def _():
        v_copy().start()

    for h in (0, 1):
        def remaining(i, carry):
            spread(node - 2 - i, h, None)
            return carry

        lax.fori_loop(0, node - 1 - jnp.maximum(blocks[h], first), remaining, 0)

    for h in range(2):
        scaled[h] = jnp.where(weights[h] > 0.0, zacc[h], 0.0)

    kept, sent = upper, 1 - upper

    def x_copy():
        target = device(node, mirror, share)
        return remote(scaled.at[sent], xrecv, x_send, x_recv, target)

    def a_copy(h):
        target = device(node, node, share)
        return remote(scaled.at[h], across.at[blocks[h], upper], a_send.at[h], a_recv.at[blocks[h], upper], target)

    def t_copy(k, half, s):
        columns = pl.ds(s * ROWS, ROWS)
        return remote(
            across.at[k, half, slice(None), columns], trecv.at[share, half],
            t_send.at[k, half, s], t_recv.at[share, half], device(k, plane, s),
        )

    def d_copy(h, s):
        return remote(
            scaled.at[h, slice(None), pl.ds(s * ROWS, ROWS)], trecv.at[share, upper],
            t_send.at[blocks[h], upper, s], t_recv.at[share, upper], device(blocks[h], node, s),
        )

    def arrival(s, half):
        tile = trecv.at[s, half]
        return remote(tile, tile, t_send.at[0, 0, 0], t_recv.at[s, half], device(plane, plane, s))

    @pl.when(node >= mirror)
    def _():
        x_copy().start()

    for h in range(2):
        @pl.when(jnp.logical_and(node > blocks[h], node <= DIRECT))
        def _():
            for s in range(SHARES):
                d_copy(h, s).start()

        @pl.when(jnp.logical_and(node > jnp.maximum(blocks[h], DIRECT), node != plane))
        def _():
            a_copy(h).start()

        @pl.when(jnp.logical_and(node > jnp.maximum(blocks[h], DIRECT), node == plane))
        def _():
            across[blocks[h], upper] = scaled[h]

    @pl.when(node >= plane)
    def _():
        out_ref[pl.ds(upper * HALF, HALF)] = scaled[kept]
        x_copy().wait_recv()
        out_ref[pl.ds((1 - upper) * HALF, HALF)] = xrecv[...]

    @pl.when(jnp.logical_and(node == plane, node > DIRECT))
    def _():
        def deal(i, carry):
            k = node - 1 - i
            for half in range(2):
                source = jnp.minimum(k, NODES - 1 - k) if half == 0 else jnp.maximum(k, NODES - 1 - k)

                @pl.when(source != plane)
                def _():
                    into = across.at[k, half]
                    remote(into, into, a_send.at[0], a_recv.at[k, half], device(node, source, share)).wait_recv()

                for s in range(SHARES):
                    t_copy(k, half, s).start()
            return carry

        lax.fori_loop(0, node, deal, 0)

    @pl.when(node < plane)
    def _():
        for s in range(SHARES):
            for half in range(2):
                arrival(s, half).wait_recv()
            tiles = jnp.concatenate([trecv[s, 0], trecv[s, 1]], 0)
            out_ref[:, s * ROWS : (s + 1) * ROWS] = tiles.T

    @pl.when(node >= mirror)
    def _():
        x_copy().wait_send()

    @pl.when(jnp.logical_and(node == plane, node > DIRECT))
    def _():
        def drain_t(k, carry):
            for half in range(2):
                for s in range(SHARES):
                    t_copy(k, half, s).wait_send()
            return carry

        lax.fori_loop(0, node, drain_t, 0)

    for kind in range(2):
        for distance in range(AHEAD + 1):
            def drained(k, slot, sub):
                y_copy(slot, sub, kind).wait_send()
                c_copy(slot, sub, 0, kind).wait_send()
                c_copy(slot, sub, 1, kind).wait_send()

            each(distance, kind, drained)
            for sub in range(CUTS):
                sends(distance, sub, kind, lambda k, slot, i, way: z_copy(slot, i, way, kind).wait_send())

    @pl.when(plane < first)
    def _():
        hand_over().wait_send()

    @pl.when(blocks[0] < first)
    def _():
        v_copy().wait_send()

    @pl.when(jnp.logical_and(node > blocks[0], jnp.logical_and(node >= 1, node <= NODES - 2 - KEPT)))
    def _():
        m_copy(node, 0, 0, None).wait_send()

    @pl.when(blocks[0] < helped)
    def _():
        s_copy().wait_send()

        def drain_early(to, carry):
            @pl.when(to != node)
            def _():
                early_copy(to).wait_send()

            return carry

        lax.fori_loop(blocks[0], helped, drain_early, 0)

    for h in range(2):
        @pl.when(node > blocks[h])
        def _():
            @pl.when(jnp.logical_and(node != plane, node > DIRECT))
            def _():
                a_copy(h).wait_send()

            @pl.when(node <= DIRECT)
            def _():
                for s in range(SHARES):
                    d_copy(h, s).wait_send()

            for sub in range(SUBS):
                p_copy(node, node - 1, h, sub).wait_send()

                @pl.when(node < NODES - 1)
                def _():
                    m_copy(node, node + 1, h, sub).wait_send()

        def drain_m(target, carry):
            m_copy(node, target, h, None).wait_send()
            return carry

        def drain_p(target, carry):
            p_copy(node, target, h, None).wait_send()
            return carry

        reach = jnp.minimum(node + KEPT + 1, NODES)
        lax.fori_loop(node + 2, jnp.where(node > blocks[h], reach, 0), drain_m, 0)
        lax.fori_loop(jnp.maximum(blocks[h], first), node - 1, drain_p, 0)


def shards(factor_panels, diag_inverse, block_lists, parent):
    f32, bf16, i32 = jnp.float32, jnp.bfloat16, jnp.int32
    dma = pltpu.SemaphoreType.DMA
    anywhere = pl.BlockSpec(memory_space=pl.ANY)
    messages = pltpu.VMEM((NODES, 2, HALF, WIDTH), f32)
    pair = pltpu.VMEM((2, HALF, WIDTH), f32)
    half = pltpu.VMEM((HALF, WIDTH), f32)
    row = pltpu.VMEM((NODES, WIDTH, WIDTH), bf16)
    block = pltpu.VMEM((WIDTH, WIDTH), bf16)
    flags = dma((NODES, 2, SUBS))
    row_cuts, cuts = dma((NODES, CUTS)), dma((NODES, CUTS, 2))
    inverse = pl.pallas_call(
        kernel,
        out_shape=jax.ShapeDtypeStruct((ROWS, WIDTH), f32),
        in_specs=[anywhere] * 4,
        out_specs=pl.BlockSpec(memory_space=pltpu.VMEM),
        scratch_shapes=[
            pltpu.VMEM((ROWS, WIDTH), f32), pltpu.VMEM((WIDTH, WIDTH), f32),
            pltpu.SMEM((NODES, NODES - 1), i32), pltpu.SMEM((NODES,), i32),
            pltpu.VMEM((NODES, SHARES, ROWS, WIDTH), f32),
            row, row, block, block, pair, messages, pair, messages, messages, half,
            messages, pltpu.VMEM((SHARES, 2, HALF, ROWS), f32),
            pair, half, half, half,
            dma((4,)), cuts, row_cuts, row_cuts, row_cuts, cuts, cuts, *[dma(())] * 6,
            flags, flags, flags, flags, dma(()), dma(()), dma((2,)), dma((NODES, 2)),
            dma((NODES, 2, SHARES)), dma((SHARES, 2)),
        ],
        compiler_params=pltpu.CompilerParams(
            collective_id=0, has_side_effects=True, vmem_limit_bytes=60 * 2**20
        ),
        name="selected_inverse",
    )(factor_panels[0], diag_inverse[0], block_lists, parent)
    return inverse[None]


def solution(mesh):
    placed = (P("prow", "pcol", None), P("prow", None, None), P(), P())
    return jax.shard_map(
        shards, mesh=mesh, in_specs=placed, out_specs=P("prow", "pcol", None), check_vma=False
    )
```

```python
import jax
import jax.numpy as jnp
from jax import lax
from jax.experimental import pallas as pl
from jax.experimental.pallas import tpu as pltpu
from jax.sharding import PartitionSpec as P

MESH = pl.DeviceIdType.MESH
NODES = 8
WIDTH = 512
SHARES = 4
ROWS = 128
HALF = ROWS // 2
SUBS = 2
CUTS = 2
PIECE = HALF // SUBS
DIRECT = 3
AHEAD, BEHIND = 4, 3
KEPT = 5
RELAY, PREPARE = 1, 2


def pattern_weight(lists_ref, parent_ref, target, node):
    found = parent_ref[target] == node
    for i in range(NODES - 1):
        found = jnp.logical_or(found, lists_ref[target, i] == node)
    return jnp.where(found, 1.0, 0.0).astype(jnp.float32)


def split(value):
    high = value.astype(jnp.bfloat16)
    low = (value - high.astype(jnp.float32)).astype(jnp.bfloat16)
    return high, low


def product(left, high_ref, low_ref, transposed):
    high, low = split(left)
    dims = (((1,), (1 if transposed else 0,)), ((), ()))
    rows = left.shape[0]
    both = lax.dot_general(
        jnp.concatenate([high, low], 0), high_ref[...], dims, preferred_element_type=jnp.float32
    )
    cross = lax.dot_general(high, low_ref[...], dims, preferred_element_type=jnp.float32)
    return both[:rows] + both[rows:] + cross


def kernel(
    f_hbm, d_hbm, lists_hbm, parent_hbm, out_ref,
    f_ref, d_ref, lists_ref, parent_ref,
    raw, lhi, llo, dhi, dlo, mine, mrecv, zacc, psend, precv, xrecv, across, trecv,
    scaled, part_sum, part_recv, solved,
    in_sem, z_send, z_recv, y_send, y_recv, c_send, c_recv,
    h_send, h_recv, s_send, s_recv, v_send, v_recv,
    m_send, m_recv, p_send, p_recv, x_send, x_recv, a_send, a_recv, t_send, t_recv,
):
    node = lax.axis_index("prow")
    col = lax.axis_index("pcol")
    plane = col // SHARES
    share = lax.rem(col, SHARES)
    y_low, core = share // 2, lax.rem(share, 2)
    y_share = (1 - y_low) * 2 + core
    c_share = y_low * 2 + 1 - core
    upper = plane // (NODES // 2)
    mirror = NODES - 1 - plane
    blocks = (jnp.minimum(plane, mirror), jnp.maximum(plane, mirror))
    first = jnp.maximum(node - KEPT, 0)
    friend = NODES - 1 - node
    helped = NODES - 1 - KEPT - node

    def device(n, z, s):
        return (n, z * SHARES + s)

    barrier = pltpu.get_barrier_semaphore()

    def greet(target):
        pl.semaphore_signal(barrier, device_id=target, device_id_type=MESH)

    for step in range(1, NODES):
        greet(device(lax.rem(node + step, NODES), plane, share))
    greet(device(node, lax.rem(plane + 1, NODES), share))
    greet(device(node, lax.rem(plane + NODES - 1, NODES), share))
    greet(device(node, mirror, share))
    greet(device(node, plane, y_share))
    greet(device(node, plane, c_share))

    @pl.when(node < plane)
    def _():
        @pl.when(plane > DIRECT)
        def _():
            for s in range(SHARES):
                greet(device(plane, plane, s))

        @pl.when(plane <= DIRECT)
        def _():
            for s in range(SHARES):
                greet(device(plane, node, s))
                greet(device(plane, NODES - 1 - node, s))

    @pl.when(jnp.logical_and(node == plane, node > DIRECT))
    def _():
        for step in range(1, NODES):
            greet(device(node, lax.rem(plane + step, NODES), share))


    @pl.when(plane < helped)
    def _():
        greet(device(friend, plane, y_share))

    loads = [
        pltpu.make_async_copy(src, dst, in_sem.at[i])
        for i, (src, dst) in enumerate(
            [(lists_hbm, lists_ref), (parent_hbm, parent_ref), (f_hbm, f_ref), (d_hbm, d_ref)]
        )
    ]
    for load in loads:
        load.start()
    for load in loads[:3]:
        load.wait()

    @pl.when(plane < node)
    def _():
        raw[plane, share] = f_ref[...] * pattern_weight(lists_ref, parent_ref, plane, node)

    for h in range(2):
        offset = share * ROWS + upper * HALF
        rows = lax.broadcasted_iota(jnp.int32, (HALF, WIDTH), 0) + offset
        columns = lax.broadcasted_iota(jnp.int32, (HALF, WIDTH), 1)
        unit = jnp.where(rows == columns, 1.0, 0.0).astype(jnp.float32)
        here = jnp.where(node == blocks[h], 1.0, 0.0).astype(jnp.float32)
        mrecv[blocks[h], h] = unit
        mine[h] = unit * here
    weights = []
    for h in range(2):
        weight = pattern_weight(lists_ref, parent_ref, blocks[h], node)
        weights.append(jnp.where(node == blocks[h], 1.0, weight))
    loads[3].wait()
    high, low = split(d_ref[...])
    dhi[...] = high
    dlo[...] = low
    relayed = jnp.where(node == plane, SHARES * node, 1)
    direct = SHARES * sum(jnp.where(node > blocks[h], 1, 0) for h in range(2))
    greeted = NODES - 1 + 5 + jnp.where(node > DIRECT, relayed, direct) + jnp.where(plane < first, 1, 0)
    pl.semaphore_wait(barrier, greeted)

    def remote(src, dst, send, recv, target):
        return pltpu.make_async_remote_copy(
            src_ref=src, dst_ref=dst, send_sem=send, recv_sem=recv,
            device_id=target, device_id_type=MESH,
        )

    def z_copy(k, sub, way, kind):
        step = 1 if way == 0 else NODES - 1
        here = raw.at[k, y_share if kind else share, pl.ds(sub * HALF, HALF)]
        target = device(node, lax.rem(plane + step, NODES), share)
        return remote(here, here, z_send.at[k, sub, way], z_recv.at[k, sub], target)

    def y_copy(k, sub, kind):
        here = raw.at[k, y_share if kind else share, pl.ds(sub * HALF, HALF)]
        target = device(node, plane, y_share)
        return remote(here, here, y_send.at[k, sub], y_recv.at[k, sub], target)

    def c_copy(k, sub, which, kind):
        here = raw.at[k, share if which == kind else y_share, pl.ds(sub * HALF, HALF)]
        target = device(node, plane, c_share)
        return remote(here, here, c_send.at[k, sub, which], c_recv.at[k, sub, which], target)

    def part(ref, index, h, sub):
        if sub is None:
            return ref.at[index, h] if index is not None else ref.at[h]
        rows = pl.ds(sub * PIECE, PIECE)
        return ref.at[index, h, rows] if index is not None else ref.at[h, rows]

    def m_copy(k, target, h, sub):
        i = sub or 0
        return remote(
            part(mine, None, h, sub), part(mrecv, k, h, sub),
            m_send.at[target, h, i], m_recv.at[k, h, i], device(target, plane, share),
        )

    def p_copy(k, target, h, sub):
        i = sub or 0
        return remote(
            part(psend, target, h, sub), part(precv, k, h, sub),
            p_send.at[target, h, i], p_recv.at[k, h, i], device(target, plane, share),
        )

    def member(k, kind):
        return k < helped if kind else jnp.logical_and(k >= first, k < node)

    def used(k, kind):
        return jnp.logical_and(member(k, kind), k >= blocks[0])

    def passes(k, way, distance, kind):
        if distance > (BEHIND if way else AHEAD):
            return False
        if way == 0:
            return jnp.logical_and(member(k, kind), k >= 2)
        return jnp.logical_and(member(k, kind), jnp.logical_or(k >= 1, distance <= 1))

    def ring(distance):
        ways = [0, 1] if distance else [0]
        return [(way, lax.rem(plane + (distance if way else NODES - distance), NODES)) for way in ways]

    def each(distance, kind, action):
        for way, k in ring(distance):
            if distance == 0 or passes(k, way, distance, kind) is not False:
                @pl.when(used(k, kind))
                def _():
                    for sub in range(CUTS):
                        action(k, k + KEPT * kind, sub)

    def sends(distance, sub, kind, action):
        for way, k in ring(distance):
            for onward in ([0, 1] if distance == 0 else [way]):
                further = passes(k, onward, distance + 1, kind)
                if further is not False:
                    @pl.when(further)
                    def _():
                        action(k, k + KEPT * kind, sub, onward)

    def land(distance, kind):
        for sub in range(CUTS):
            for way, k in ring(distance):
                arrives = passes(k, way, distance, kind) if distance else False
                if arrives is not False:
                    @pl.when(arrives)
                    def _():
                        z_copy(k + KEPT * kind, sub, way, kind).wait_recv()

            sends(distance, sub, kind, lambda k, slot, i, way: z_copy(slot, i, way, kind).start())
            for way, k in ring(distance):
                if distance == 0 or passes(k, way, distance, kind) is not False:
                    @pl.when(used(k, kind))
                    def _():
                        y_copy(k + KEPT * kind, sub, kind).start()
                        c_copy(k + KEPT * kind, sub, 0, kind).start()

    def relay(distance, kind):
        def action(k, slot, sub):
            y_copy(slot, sub, kind).wait_recv()
            c_copy(slot, sub, 1, kind).start()

        each(distance, kind, action)

    def prepare(k, slot, sub, kind):
        c_copy(slot, sub, 0, kind).wait_recv()
        c_copy(slot, sub, 1, kind).wait_recv()
        for i in range(SHARES):
            high, low = split(raw[slot, i, sub * HALF : (sub + 1) * HALF])
            rows = slice(i * ROWS + sub * HALF, i * ROWS + (sub + 1) * HALF)
            lhi[slot, rows] = high
            llo[slot, rows] = low

    def gather(kind):
        for step in range(AHEAD + 1 + PREPARE):
            if step <= AHEAD:
                land(step, kind)
            if 0 <= step - RELAY <= AHEAD:
                relay(step - RELAY, kind)
            if 0 <= step - PREPARE <= AHEAD:
                each(step - PREPARE, kind, lambda k, slot, sub: prepare(k, slot, sub, kind))

    def hand_over():
        target = device(friend, plane, y_share)
        return remote(raw.at[plane, share], raw.at[plane + KEPT, share], h_send, h_recv, target)

    @pl.when(plane < first)
    def _():
        hand_over().start()

    gather(0)

    def forward(k, carry):
        for h in range(2):
            @pl.when(k >= blocks[h])
            def _():
                @pl.when(k > blocks[h])
                def _():
                    m_copy(k, node, h, None).wait_recv()

                mine[h] = mine[h] - product(mrecv[k, h], lhi.at[k], llo.at[k], True)

        return carry

    lax.fori_loop(first, node - 1, forward, 0)

    def s_copy():
        return remote(part_sum, part_recv, s_send, s_recv, device(friend, plane, share))

    @pl.when(blocks[0] < first)
    def _():
        s_copy().wait_recv()
        mine[0] = mine[0] - part_recv[...]

    for h in range(2):
        @pl.when(node > blocks[h])
        def _():
            last = node - 1
            for sub in range(SUBS):
                @pl.when(last > blocks[h])
                def _():
                    m_copy(last, node, h, sub).wait_recv()

                rows = slice(sub * PIECE, (sub + 1) * PIECE)
                mine[h, rows] = mine[h, rows] - product(
                    mrecv[last, h, rows], lhi.at[last], llo.at[last], True
                )

                @pl.when(node < NODES - 1)
                def _():
                    m_copy(node, node + 1, h, sub).start()

            def body(target, carry):
                m_copy(node, target, h, None).start()
                return carry

            lax.fori_loop(node + 2, jnp.minimum(node + KEPT + 1, NODES), body, 0)

    @pl.when(jnp.logical_and(node > blocks[0], jnp.logical_and(node >= 1, node <= NODES - 2 - KEPT)))
    def _():
        m_copy(node, 0, 0, None).start()
        mrecv[node, 0] = mine[0]

    @pl.when(plane < helped)
    def _():
        remote(raw.at[0, 0], raw.at[0, 0], h_send, h_recv, device(friend, plane, y_share)).wait_recv()

    gather(1)

    @pl.when(blocks[0] < helped)
    def _():
        part_sum[...] = jnp.zeros_like(part_sum)

        def term(k, carry):
            @pl.when(jnp.logical_and(k > blocks[0], k != node))
            def _():
                m_copy(k, node, 0, None).wait_recv()

            part_sum[...] += product(mrecv[k, 0], lhi.at[k + KEPT], llo.at[k + KEPT], True)
            return carry

        lax.fori_loop(blocks[0], helped, term, 0)
        s_copy().start()

    def v_copy():
        return remote(zacc.at[0], solved, v_send, v_recv, device(friend, plane, share))

    def early_copy(to):
        return remote(
            psend.at[to + KEPT, 0], precv.at[friend, 0],
            p_send.at[to + KEPT, 0, 0], p_recv.at[friend, 0, 0], device(to, plane, share),
        )

    @pl.when(blocks[0] < helped)
    def _():
        v_copy().wait_recv()

        def early(to, carry):
            psend[to + KEPT, 0] = product(solved[...], lhi.at[to + KEPT], llo.at[to + KEPT], False)

            @pl.when(to != node)
            def _():
                early_copy(to).start()

            @pl.when(to == node)
            def _():
                precv[friend, 0] = psend[to + KEPT, 0]

            return carry

        lax.fori_loop(blocks[0], helped, early, 0)

    def collect(k, h, sub):
        if h == 0 and sub is None:
            @pl.when(jnp.logical_not(jnp.logical_and(k == friend, node < helped)))
            def _():
                p_copy(k, node, h, sub).wait_recv()
        else:
            p_copy(k, node, h, sub).wait_recv()
        rows = slice(0, HALF) if sub is None else slice(sub * PIECE, (sub + 1) * PIECE)
        zacc[h, rows] = zacc[h, rows] - precv[k, h, rows]

    def spread(to, h, sub):
        rows = slice(0, HALF) if sub is None else slice(sub * PIECE, (sub + 1) * PIECE)
        psend[to, h, rows] = product(zacc[h, rows], lhi.at[to], llo.at[to], False)
        p_copy(node, to, h, sub).start()

    for h in (0, 1):
        @pl.when(node >= blocks[h])
        def _():
            zacc[h] = product(mine[h], dhi, dlo, False)

            def backward(i, carry):
                collect(NODES - 1 - i, h, None)
                return carry

            lax.fori_loop(0, NODES - 2 - node, backward, 0)
            for sub in range(SUBS):
                @pl.when(node < NODES - 1)
                def _():
                    collect(node + 1, h, sub)

                @pl.when(node > blocks[h])
                def _():
                    spread(node - 1, h, sub)

    @pl.when(blocks[0] < first)
    def _():
        v_copy().start()

    for h in (0, 1):
        def remaining(i, carry):
            spread(node - 2 - i, h, None)
            return carry

        lax.fori_loop(0, node - 1 - jnp.maximum(blocks[h], first), remaining, 0)

    for h in range(2):
        scaled[h] = jnp.where(weights[h] > 0.0, zacc[h], 0.0)

    kept, sent = upper, 1 - upper

    def x_copy(sub):
        target = device(node, mirror, share)
        rows = pl.ds(sub * PIECE, PIECE)
        return remote(scaled.at[sent, rows], xrecv.at[rows], x_send.at[sub], x_recv.at[sub], target)

    def a_copy(h):
        target = device(node, node, share)
        return remote(scaled.at[h], across.at[blocks[h], upper], a_send.at[h], a_recv.at[blocks[h], upper], target)

    def t_copy(k, half, s):
        columns = pl.ds(s * ROWS, ROWS)
        return remote(
            across.at[k, half, slice(None), columns], trecv.at[share, half],
            t_send.at[k, half, s], t_recv.at[share, half], device(k, plane, s),
        )

    def d_copy(h, s):
        return remote(
            scaled.at[h, slice(None), pl.ds(s * ROWS, ROWS)], trecv.at[share, upper],
            t_send.at[blocks[h], upper, s], t_recv.at[share, upper], device(blocks[h], node, s),
        )

    def arrival(s, half):
        tile = trecv.at[s, half]
        return remote(tile, tile, t_send.at[0, 0, 0], t_recv.at[s, half], device(plane, plane, s))

    @pl.when(node >= mirror)
    def _():
        for sub in range(SUBS):
            x_copy(sub).start()

    for h in range(2):
        @pl.when(jnp.logical_and(node > blocks[h], node <= DIRECT))
        def _():
            for s in range(SHARES):
                d_copy(h, s).start()

        @pl.when(jnp.logical_and(node > jnp.maximum(blocks[h], DIRECT), node != plane))
        def _():
            a_copy(h).start()

        @pl.when(jnp.logical_and(node > jnp.maximum(blocks[h], DIRECT), node == plane))
        def _():
            across[blocks[h], upper] = scaled[h]

    @pl.when(node >= plane)
    def _():
        out_ref[pl.ds(upper * HALF, HALF)] = scaled[kept]
        for sub in range(SUBS):
            x_copy(sub).wait_recv()
            out_ref[pl.ds((1 - upper) * HALF + sub * PIECE, PIECE)] = xrecv[sub * PIECE : (sub + 1) * PIECE]

    @pl.when(jnp.logical_and(node == plane, node > DIRECT))
    def _():
        def deal(i, carry):
            k = node - 1 - i
            for half in range(2):
                source = jnp.minimum(k, NODES - 1 - k) if half == 0 else jnp.maximum(k, NODES - 1 - k)

                @pl.when(source != plane)
                def _():
                    into = across.at[k, half]
                    remote(into, into, a_send.at[0], a_recv.at[k, half], device(node, source, share)).wait_recv()

                for s in range(SHARES):
                    t_copy(k, half, s).start()
            return carry

        lax.fori_loop(0, node, deal, 0)

    @pl.when(node < plane)
    def _():
        for s in range(SHARES):
            for half in range(2):
                arrival(s, half).wait_recv()
            tiles = jnp.concatenate([trecv[s, 0], trecv[s, 1]], 0)
            out_ref[:, s * ROWS : (s + 1) * ROWS] = tiles.T

    @pl.when(node >= mirror)
    def _():
        for sub in range(SUBS):
            x_copy(sub).wait_send()

    @pl.when(jnp.logical_and(node == plane, node > DIRECT))
    def _():
        def drain_t(k, carry):
            for half in range(2):
                for s in range(SHARES):
                    t_copy(k, half, s).wait_send()
            return carry

        lax.fori_loop(0, node, drain_t, 0)

    for kind in range(2):
        for distance in range(AHEAD + 1):
            def drained(k, slot, sub):
                y_copy(slot, sub, kind).wait_send()
                c_copy(slot, sub, 0, kind).wait_send()
                c_copy(slot, sub, 1, kind).wait_send()

            each(distance, kind, drained)
            for sub in range(CUTS):
                sends(distance, sub, kind, lambda k, slot, i, way: z_copy(slot, i, way, kind).wait_send())

    @pl.when(plane < first)
    def _():
        hand_over().wait_send()

    @pl.when(blocks[0] < first)
    def _():
        v_copy().wait_send()

    @pl.when(jnp.logical_and(node > blocks[0], jnp.logical_and(node >= 1, node <= NODES - 2 - KEPT)))
    def _():
        m_copy(node, 0, 0, None).wait_send()

    @pl.when(blocks[0] < helped)
    def _():
        s_copy().wait_send()

        def drain_early(to, carry):
            @pl.when(to != node)
            def _():
                early_copy(to).wait_send()

            return carry

        lax.fori_loop(blocks[0], helped, drain_early, 0)

    for h in range(2):
        @pl.when(node > blocks[h])
        def _():
            @pl.when(jnp.logical_and(node != plane, node > DIRECT))
            def _():
                a_copy(h).wait_send()

            @pl.when(node <= DIRECT)
            def _():
                for s in range(SHARES):
                    d_copy(h, s).wait_send()

            for sub in range(SUBS):
                p_copy(node, node - 1, h, sub).wait_send()

                @pl.when(node < NODES - 1)
                def _():
                    m_copy(node, node + 1, h, sub).wait_send()

        def drain_m(target, carry):
            m_copy(node, target, h, None).wait_send()
            return carry

        def drain_p(target, carry):
            p_copy(node, target, h, None).wait_send()
            return carry

        reach = jnp.minimum(node + KEPT + 1, NODES)
        lax.fori_loop(node + 2, jnp.where(node > blocks[h], reach, 0), drain_m, 0)
        lax.fori_loop(jnp.maximum(blocks[h], first), node - 1, drain_p, 0)


def shards(factor_panels, diag_inverse, block_lists, parent):
    f32, bf16, i32 = jnp.float32, jnp.bfloat16, jnp.int32
    dma = pltpu.SemaphoreType.DMA
    anywhere = pl.BlockSpec(memory_space=pl.ANY)
    messages = pltpu.VMEM((NODES, 2, HALF, WIDTH), f32)
    pair = pltpu.VMEM((2, HALF, WIDTH), f32)
    half = pltpu.VMEM((HALF, WIDTH), f32)
    row = pltpu.VMEM((NODES, WIDTH, WIDTH), bf16)
    block = pltpu.VMEM((WIDTH, WIDTH), bf16)
    flags = dma((NODES, 2, SUBS))
    row_cuts, cuts = dma((NODES, CUTS)), dma((NODES, CUTS, 2))
    inverse = pl.pallas_call(
        kernel,
        out_shape=jax.ShapeDtypeStruct((ROWS, WIDTH), f32),
        in_specs=[anywhere] * 4,
        out_specs=pl.BlockSpec(memory_space=pltpu.VMEM),
        scratch_shapes=[
            pltpu.VMEM((ROWS, WIDTH), f32), pltpu.VMEM((WIDTH, WIDTH), f32),
            pltpu.SMEM((NODES, NODES - 1), i32), pltpu.SMEM((NODES,), i32),
            pltpu.VMEM((NODES, SHARES, ROWS, WIDTH), f32),
            row, row, block, block, pair, messages, pair, messages, messages, half,
            messages, pltpu.VMEM((SHARES, 2, HALF, ROWS), f32),
            pair, half, half, half,
            dma((4,)), cuts, row_cuts, row_cuts, row_cuts, cuts, cuts, *[dma(())] * 6,
            flags, flags, flags, flags, dma((SUBS,)), dma((SUBS,)), dma((2,)), dma((NODES, 2)),
            dma((NODES, 2, SHARES)), dma((SHARES, 2)),
        ],
        compiler_params=pltpu.CompilerParams(
            collective_id=0, has_side_effects=True, vmem_limit_bytes=60 * 2**20
        ),
        name="selected_inverse",
    )(factor_panels[0], diag_inverse[0], block_lists, parent)
    return inverse[None]


def solution(mesh):
    placed = (P("prow", "pcol", None), P("prow", None, None), P(), P())
    return jax.shard_map(
        shards, mesh=mesh, in_specs=placed, out_specs=P("prow", "pcol", None), check_vma=False
    )
```
